256 devices in a mesh: half: 2 (over z_lo), row: 8 (over z_hi, core), col: 16 (over y, x).
Axes of the slice: x: 4, y: 4, z: 8 (z_hi: 4, z_lo: 2; z = z_hi * 2 + z_lo), core: 2. Of those that a mesh axis runs over, the one named last changes fastest.
Arguments:
- root_factor: bfloat16 [3, 16, 128, 3, 16, 128], P(None, ('half', 'row'), None, None, 'col')
- root_pivots: float32 [3, 16, 128], P(None, ('half', 'row')), may hold values from -2 to 2
- child_factor: bfloat16 [2, 4, 8, 128, 2, 16, 128], P('half', None, 'row', None, None, 'col')
- child_pivots: float32 [2, 4, 8, 128], P('half', None, 'row'), may hold values from -2 to 2
- child_block: bfloat16 [2, 6, 8, 64, 2, 16, 128], P('half', None, 'row', None, None, 'col'), may hold values from -0.109375 to 0.109375
- child_rows: int32 [2, 3072], P('half'), may hold values from 0 to 6143, as said below
Outputs:
- root_inverse: float32 [6, 8, 128, 3, 16, 128], P(None, 'row', None, None, 'col')
- child_offdiag: float32 [2, 6, 8, 64, 2, 16, 128], P('half', None, 'row', None, None, 'col')
- child_inverse: float32 [2, 4, 8, 128, 2, 16, 128], P('half', None, 'row', None, None, 'col')
The draws below stay inside these ranges and needn't reach their ends.
Inputs may be any that keep to these rules, and one draw needn't show every extreme that they name: root_factor read as a 6144 x 6144 matrix and each child_factor[c] read as a 4096 x 4096 matrix are unit lower triangular (ones on the diagonal, zeros above it). Entry i of child_rows[c] lies in root rows 128 * k to 128 * k + 127 for k = i // 64; every such block contributes its first and its last row; entries of one child are distinct and ascending.
All inputs are finite; a program needn't handle non-finite values.
Results may differ from the reference program's by a relative error of at most 0.0041.
Values may be sent and summed in bfloat16 or wider, within the bound.
No kernel may reach another device: no remote copies, remote signals or barrier semaphores. Data moves between devices by JAX's collectives and lax.ppermute only.
A program may use at most 128 MiB of HBM per device.

```python
import math
import jax
import jax.numpy as jnp
from jax import lax

BLK = 128
NR = 6144
NC = 4096
NS = 3072
REACH = 64
N_HALF = 2
N_ROW = 8
N_COL = 16


def unit_lower(raw, scale):
    lower = lax.broadcasted_iota(jnp.int32, raw.shape, raw.ndim - 2)
    upper = lax.broadcasted_iota(jnp.int32, raw.shape, raw.ndim - 1)
    diagonal = jnp.where(lower == upper, 1.0, 0.0).astype(jnp.float32)
    return jnp.where(lower > upper, raw * scale, diagonal).astype(jnp.bfloat16)


def draw_root_factor(key, part):
    key = jax.random.fold_in(key, 11)
    raw = jax.random.normal(key, (NR, NR), jnp.float32)
    whole = unit_lower(raw, 2.0 / math.sqrt(NR))
    return whole.reshape(NR // (BLK * N_HALF * N_ROW), N_HALF * N_ROW, BLK, NR // (BLK * N_COL), N_COL, BLK)


def draw_child_factor(key, part):
    key = jax.random.fold_in(key, 23)
    raw = jax.random.normal(key, (2, NC, NC), jnp.float32)
    whole = unit_lower(raw, 2.0 / math.sqrt(NC))
    return whole.reshape(2, NC // (BLK * N_ROW), N_ROW, BLK, NC // (BLK * N_COL), N_COL, BLK)


def draw_child_rows(key, part):
    key = jax.random.fold_in(key, 37)
    span = BLK
    take = REACH
    blocks = NR // BLK
    keys = jax.random.split(key, 2 * blocks)

    def pick(single):
        inner = jax.random.permutation(single, span - 2).astype(jnp.int32) + 1
        chosen = jnp.sort(inner[:take - 2])
        first = jnp.zeros((1,), jnp.int32)
        final = jnp.full((1,), span - 1, jnp.int32)
        return jnp.concatenate([first, chosen, final])
    offsets = jax.vmap(pick)(keys).reshape(2, blocks, take)
    base = (jnp.arange(blocks, dtype=jnp.int32) * span)[None, :, None]
    return (offsets + base).reshape(2, NS).astype(jnp.int32)


def block_levels(own_key, shape, shards, low, top_value):
    def one(axis_at, parts):
        heights = jax.random.uniform(jax.random.fold_in(jax.random.fold_in(own_key, 6), axis_at), (parts,), jnp.float32, low / len(shards), top_value / len(shards))
        return jnp.repeat(jnp.exp(heights), shape[axis_at] // parts).reshape((-1,) + (1,) * (len(shape) - axis_at - 1))

    loudness = one(*shards[0])
    for cut in shards[1:]:
        loudness = loudness * one(*cut)
    return loudness


def normal_values(key, shape, spread, bound, shards=(), kind=jnp.bfloat16):
    result = jax.random.normal(key, shape, jnp.float32) * spread
    if len(shards) > 0:
        result = block_levels(key, shape, shards, -0.22, 0.18) * result
    return jnp.clip(result, min=-bound, max=bound).astype(kind)


def setup_inputs(seed: int = 0) -> dict:
    streams_of = jax.random.split(jax.random.key(seed), 7)
    root_factor = draw_root_factor(jax.random.fold_in(streams_of[6], 71), 0)
    root_pivots = jnp.clip(jax.random.uniform(streams_of[1], (NR // (BLK * N_HALF * N_ROW), N_HALF * N_ROW, BLK), jnp.float32, -2.0, 2.0) * block_levels(streams_of[1], (NR // (BLK * N_HALF * N_ROW), N_HALF * N_ROW, BLK), ((1, 16),), -0.4, 0.0), -2.0, 2.0)
    child_factor = draw_child_factor(jax.random.fold_in(streams_of[6], 71), 0)
    child_pivots = jnp.clip(jax.random.uniform(streams_of[3], (2, NC // (BLK * N_ROW), N_ROW, BLK), jnp.float32, -2.0, 2.0) * block_levels(streams_of[3], (2, NC // (BLK * N_ROW), N_ROW, BLK), ((0, 2), (2, 8)), -0.4, 0.0), -2.0, 2.0)
    child_block = normal_values(streams_of[4], (2, NS // (REACH * N_ROW), N_ROW, REACH, NC // (BLK * N_COL), N_COL, BLK), NS ** -0.5, 0.109375, ((0, 2), (2, 8), (5, 16)))
    child_rows = draw_child_rows(jax.random.fold_in(streams_of[6], 71), 0)
    return {"root_factor": root_factor, "root_pivots": root_pivots, "child_factor": child_factor, "child_pivots": child_pivots, "child_block": child_block, "child_rows": child_rows}


def transpose_product(left, right):
    return lax.dot_general(left.astype(jnp.float32), right.astype(jnp.float32), (((0,), (0,)), ((), ())), precision=lax.Precision.HIGHEST, preferred_element_type=jnp.float32)


def plain_product(left, right):
    return jnp.dot(left.astype(jnp.float32), right.astype(jnp.float32), precision=lax.Precision.HIGHEST, preferred_element_type=jnp.float32)


def reference(root_factor, root_pivots, child_factor, child_pivots, child_block, child_rows):
    factor = root_factor.reshape(NR, NR)
    pivots = root_pivots.reshape(NR)
    scaled_root = (pivots[:, None] * factor.astype(jnp.float32)).astype(jnp.bfloat16)
    whole_inverse = transpose_product(factor, scaled_root)
    root_low = whole_inverse.astype(jnp.bfloat16)
    lowers = child_factor.reshape(2, NC, NC)
    scales = child_pivots.reshape(2, NC)
    couplings = child_block.reshape(2, NS, NC)
    offdiags = []
    inverses = []
    for child in range(2):
        rows = child_rows[child].astype(jnp.int32)
        restricted = jnp.take(jnp.take(root_low, rows, axis=0), rows, axis=1)
        offdiag = -plain_product(restricted, couplings[child])
        offdiag_low = offdiag.astype(jnp.bfloat16)
        scaled_child = (scales[child][:, None] * lowers[child].astype(jnp.float32)).astype(jnp.bfloat16)
        inverse = transpose_product(lowers[child], scaled_child) - transpose_product(couplings[child], offdiag_low)
        offdiags.append(offdiag)
        inverses.append(inverse)
    root_inverse = whole_inverse.reshape(NR // (BLK * N_ROW), N_ROW, BLK, NR // (BLK * N_COL), N_COL, BLK)
    child_offdiag = jnp.stack(offdiags).reshape(2, NS // (REACH * N_ROW), N_ROW, REACH, NC // (BLK * N_COL), N_COL, BLK)
    child_inverse = jnp.stack(inverses).reshape(2, NC // (BLK * N_ROW), N_ROW, BLK, NC // (BLK * N_COL), N_COL, BLK)
    return root_inverse, child_offdiag, child_inverse
```

```python
import functools

import jax
import jax.numpy as jnp
from jax import lax
from jax.experimental import pallas as pl
from jax.experimental.pallas import tpu as pltpu
from jax.sharding import PartitionSpec as P

AXES = ("half", "row", "col")
N_HALF, N_ROW, N_COL = 2, 8, 16
SIDE = 4
BLK = 128
REACH = 64
VMEM_LIMIT = 48 * 1024 * 1024


def permute(array, target):
    pairs = []
    for half in range(N_HALF):
        for row in range(N_ROW):
            for col in range(N_COL):
                to_half, to_row, to_col = target(half, row, col)
                pairs.append(
                    (
                        (half * N_ROW + row) * N_COL + col,
                        (to_half * N_ROW + to_row) * N_COL + to_col,
                    )
                )
    return lax.ppermute(array, AXES, pairs)


def along_x(step):
    return lambda h, r, q: (h, r, q // SIDE * SIDE + (q + step) % SIDE)


def along_y(step):
    return lambda h, r, q: (h, r, (q + SIDE * step) % N_COL)


def along_z(step):
    return lambda h, r, q: (h, (r + 2 * step) % N_ROW, q)


def other_core(h, r, q):
    return (h, r ^ 1, q)


def other_half(h, r, q):
    return (1 - h, r, q)


def transposed_place(h, r, q):
    return (h, q % N_ROW, q // N_ROW * N_ROW + (r ^ (q % N_ROW)))


def ring_gather(own, along, split):
    before = permute(own, along(1))
    after = permute(own, along(-1))
    if split:
        cut = own.shape[0] // 2
        across = jnp.concatenate(
            [permute(before[:cut], along(1)), permute(after[cut:], along(-1))], 0
        )
    else:
        across = permute(before, along(1))
    return jnp.concatenate([own, after, across, before], 0)


def plane_gather(first, second):
    one = ring_gather(first, along_x, False)
    two = ring_gather(second, along_y, False)
    one = ring_gather(one, along_y, True)
    two = ring_gather(two, along_x, True)
    return one.reshape(N_COL, *first.shape), two.reshape(N_COL, *second.shape)


def dot(left, right):
    return jnp.dot(left, right, preferred_element_type=jnp.float32)


def dot_nt(left, right):
    return lax.dot_general(left, right, (((1,), (1,)), ((), ())), preferred_element_type=jnp.float32)


def cat(parts, axis):
    return jnp.concatenate(parts, axis)


def root_kernel(slot_one, slot_two, one_ref, two_ref, right_ref, out_ref, acc):
    acc[...] = jnp.zeros_like(acc)

    def step(r, carry):
        right = [right_ref[r, pl.ds(BLK * i, BLK), :] for i in range(6)]
        right_0 = right[0]
        right_1 = cat(right[1:3], 1)
        right_2 = cat(right[3:6], 1)
        for side in range(2):
            one = slot_one[side * N_ROW + r]
            two = slot_two[side * N_ROW + r]
            acc[side] += dot(two_ref[two], right_2)
            acc[side, : 2 * BLK, : 2 * BLK] += dot(one_ref[one, BLK:, :], right_1)
            acc[side, :BLK, :BLK] += dot(one_ref[one, :BLK, :], right_0)
        return carry

    lax.fori_loop(0, N_ROW, step, 0)
    for outer in range(3):
        for side in range(2):
            out_ref[pl.ds((2 * outer + side) * BLK, BLK), :] = acc[
                side, pl.ds(outer * BLK, BLK), :
            ].astype(out_ref.dtype)


def pick_kernel(mine_ref, other_ref, row_ref, col_ref, root_ref, picked_ref):
    total = mine_ref[...].astype(jnp.float32) + other_ref[...].astype(jnp.float32)
    root_ref[...] = total
    low = total.astype(jnp.bfloat16)
    lanes = lax.broadcasted_iota(jnp.int32, (REACH, BLK), 1)

    def chooser(ref, i):
        return jnp.where(ref[pl.ds(i * REACH, REACH), :] == lanes, 1.0, 0.0).astype(jnp.bfloat16)

    rows = cat(
        [dot(chooser(row_ref, i), low[i * BLK : (i + 1) * BLK, :]).astype(jnp.bfloat16) for i in range(6)], 0
    )
    for i in range(3):
        picked_ref[pl.ds(i * REACH, REACH), :] = dot_nt(
            chooser(col_ref, i), rows[:, i * BLK : (i + 1) * BLK]
        ).astype(jnp.bfloat16)


def offdiag_kernel(slot_one, slot_two, one_ref, two_ref, block_ref, out_ref, low_ref, acc):
    acc[...] = jnp.zeros_like(acc)

    def step(r, carry):
        left = cat([block_ref[r, pl.ds(256 * i, 256), :] for i in range(3)], 1)
        right = cat(
            [
                one_ref[slot_one[r]],
                two_ref[slot_two[r]],
                one_ref[slot_one[N_ROW + r]],
                two_ref[slot_two[N_ROW + r]],
            ],
            0,
        )
        acc[...] += dot(left, right)
        return carry

    lax.fori_loop(0, N_ROW, step, 0)
    total = -acc[...]
    low_ref[...] = total.astype(low_ref.dtype)
    out_ref[...] = total.T


def own_kernel(slots, left_ref, right_ref, out_ref, acc):
    acc[...] = jnp.zeros_like(acc)

    def step(r, carry):
        right = [right_ref[r, pl.ds(BLK * i, BLK), :] for i in range(6)]
        right_0 = cat(right[0:2], 0)
        right_1 = cat([cat(right[2:4], 1), cat(right[4:6], 1)], 0)
        for side in range(2):
            slot = slots[side * N_ROW + r]
            left_0 = cat([left_ref[slot, :BLK, :], left_ref[slot, BLK : 2 * BLK, :]], 1)
            left_1 = cat([left_ref[slot, 2 * BLK : 4 * BLK, :], left_ref[slot, 4 * BLK : 6 * BLK, :]], 1)
            acc[side] += dot(left_1, right_1)
            acc[side, :BLK, :BLK] += dot(left_0, right_0)
        return carry

    lax.fori_loop(0, N_ROW, step, 0)
    out_ref[...] = acc[...]


def child_kernel(slots, part_slots, own_ref, left_ref, right_ref, out_ref, acc):
    acc[...] = own_ref[...]

    def step(r, carry):
        right = right_ref[part_slots[r]]
        for side in range(2):
            slot = slots[side * N_ROW + r]
            left = cat([left_ref[slot, pl.ds(256 * i, 256), :] for i in range(3)], 1)
            acc[side] -= dot_nt(left, right)
        return carry

    lax.fori_loop(0, N_ROW, step, 0)
    for outer in range(2):
        for side in range(2):
            out_ref[pl.ds((2 * outer + side) * BLK, BLK), :] = acc[side, pl.ds(outer * BLK, BLK), :]


def call(kernel, scalars, arrays, outs, scratch=(), blocks=None):
    vmem = pl.BlockSpec(memory_space=pltpu.VMEM)
    smem = pl.BlockSpec(memory_space=pltpu.SMEM)
    return pl.pallas_call(
        kernel,
        in_specs=[smem] * len(scalars) + [vmem] * len(arrays),
        out_specs=[vmem] * len(outs),
        out_shape=[jax.ShapeDtypeStruct(*o) for o in outs],
        scratch_shapes=list(scratch),
        compiler_params=pltpu.CompilerParams(vmem_limit_bytes=VMEM_LIMIT),
    )(*scalars, *arrays)


def stack_blocks(array, pairs):
    return jnp.concatenate([array[a, :, b, :] for a, b in pairs], 0)


def per_device(root_factor, root_pivots, child_factor, child_pivots, child_block, child_rows):
    row = lax.axis_index("row")
    col = lax.axis_index("col")
    bf16 = jnp.bfloat16
    root = root_factor.reshape(3, BLK, 3, BLK)
    scaled_root = (root_pivots.reshape(3, BLK, 1, 1) * root.astype(jnp.float32)).astype(bf16)
    root_pairs = [(0, 0), (1, 0), (1, 1), (2, 0), (2, 1), (2, 2)]
    root_turned = stack_blocks(root.transpose(0, 3, 2, 1), root_pairs)
    root_scaled = stack_blocks(scaled_root, root_pairs)

    child = child_factor.reshape(4, BLK, 2, BLK)
    scaled_child = (child_pivots.reshape(4, BLK, 1, 1) * child.astype(jnp.float32)).astype(bf16)
    child_pairs = [(0, 0), (1, 0), (2, 0), (2, 1), (3, 0), (3, 1)]
    child_turned = stack_blocks(child.transpose(0, 3, 2, 1), child_pairs)
    child_scaled = stack_blocks(scaled_child, child_pairs)
    block = child_block.reshape(6 * REACH, 2 * BLK)
    block_turned = block.T.reshape(2 * BLK, 3, BLK).transpose(1, 0, 2).reshape(768, BLK)
    block_sorted = block.reshape(3, 2, REACH, 2 * BLK).transpose(1, 0, 2, 3).reshape(6 * REACH, 2 * BLK)
    block_sorted = block_sorted.T.reshape(2 * BLK, 3, BLK).transpose(1, 0, 2).reshape(768, BLK)

    root_right = lax.all_gather(root_scaled, "row", axis=0, tiled=False)
    root_here = permute(root_turned, transposed_place)
    child_here = permute(jnp.concatenate([child_turned, block_turned], 0), transposed_place)
    child_left = lax.all_gather(child_here, "col", axis=0, tiled=False)
    child_right = lax.all_gather(jnp.concatenate([child_scaled, block_sorted], 0), "row", axis=0, tiled=False)

    root_one, root_two = plane_gather(root_here[:384], root_here[384:])

    side = jnp.arange(2, dtype=jnp.int32)[:, None]
    classes = jnp.arange(N_ROW, dtype=jnp.int32)[None, :]
    source = side * N_ROW + (classes ^ row)
    my_x, my_y = col % SIDE, col // SIDE

    def plane_slots(place):
        dx = (place % SIDE - my_x) % SIDE
        dy = (place // SIDE - my_y) % SIDE
        return (dy * SIDE + dx).reshape(-1), (dx * SIDE + dy).reshape(-1)

    root_slots = plane_slots(source)
    (partial,) = call(
        root_kernel,
        root_slots,
        (root_one, root_two, root_right),
        [((768, 384), bf16)],
        [pltpu.VMEM((2, 384, 384), jnp.float32)],
    )
    other = permute(partial, other_half)
    rows = child_rows[0].reshape(48, REACH) % BLK
    row_picks = lax.dynamic_index_in_dim(rows.reshape(6, N_ROW, REACH), row, 1, keepdims=False)
    col_picks = lax.dynamic_index_in_dim(rows.reshape(3, N_COL, REACH), col, 1, keepdims=False)
    root_inverse, picked = call(
        pick_kernel,
        (),
        (partial, other, row_picks.reshape(-1, 1), col_picks.reshape(-1, 1)),
        [((768, 384), jnp.float32), ((192, 384), bf16)],
    )
    restricted_one, restricted_two = plane_gather(picked[:96], picked[96:])
    offdiag_slots = plane_slots(side * N_ROW + classes)
    offdiag, offdiag_low = call(
        offdiag_kernel,
        offdiag_slots,
        (restricted_one, restricted_two, child_right[:, 768:]),
        [((384, 256), jnp.float32), ((256, 384), bf16)],
        [pltpu.VMEM((256, 384), jnp.float32)],
    )
    slots = source.reshape(-1)
    (own,) = call(
        own_kernel,
        (slots,),
        (child_left[:, :768], child_right[:, :768]),
        [((2, 256, 256), jnp.float32)],
        [pltpu.VMEM((2, 256, 256), jnp.float32)],
    )
    line = ring_gather(offdiag_low, along_z, True)
    beside = permute(line, other_core)
    parts = jnp.concatenate([line, beside], 0).reshape(N_ROW, 256, 384)
    r = classes[0]
    part_slots = ((r ^ row) & 1) * SIDE + (r // 2 - row // 2) % SIDE
    (child_inverse,) = call(
        child_kernel,
        (slots, part_slots),
        (own, child_left[:, 768:], parts),
        [((512, 256), jnp.float32)],
        [pltpu.VMEM((2, 256, 256), jnp.float32)],
    )
    return (
        root_inverse.reshape(6, 1, BLK, 3, 1, BLK),
        offdiag.reshape(child_block.shape),
        child_inverse.reshape(child_factor.shape),
    )


def solution(mesh):
    return jax.shard_map(
        per_device,
        mesh=mesh,
        in_specs=(
            P(None, ("half", "row"), None, None, "col", None),
            P(None, ("half", "row"), None),
            P("half", None, "row", None, None, "col", None),
            P("half", None, "row", None),
            P("half", None, "row", None, None, "col", None),
            P("half", None),
        ),
        out_specs=(
            P(None, "row", None, None, "col", None),
            P("half", None, "row", None, None, "col", None),
            P("half", None, "row", None, None, "col", None),
        ),
        check_vma=False,
    )
```

```python
import functools

import jax
import jax.numpy as jnp
from jax import lax
from jax.experimental import pallas as pl
from jax.experimental.pallas import tpu as pltpu
from jax.sharding import PartitionSpec as P

AXES = ("half", "row", "col")
N_HALF, N_ROW, N_COL = 2, 8, 16
SIDE = 4
BLK = 128
REACH = 64
VMEM_LIMIT = 48 * 1024 * 1024


def permute(array, target):
    pairs = []
    for half in range(N_HALF):
        for row in range(N_ROW):
            for col in range(N_COL):
                to_half, to_row, to_col = target(half, row, col)
                pairs.append(
                    (
                        (half * N_ROW + row) * N_COL + col,
                        (to_half * N_ROW + to_row) * N_COL + to_col,
                    )
                )
    return lax.ppermute(array, AXES, pairs)


def along_x(step):
    return lambda h, r, q: (h, r, q // SIDE * SIDE + (q + step) % SIDE)


def along_y(step):
    return lambda h, r, q: (h, r, (q + SIDE * step) % N_COL)


def along_z(step):
    return lambda h, r, q: (h, (r + 2 * step) % N_ROW, q)


def other_core(h, r, q):
    return (h, r ^ 1, q)


def other_half(h, r, q):
    return (1 - h, r, q)


def transposed_place(h, r, q):
    return (h, q % N_ROW, q // N_ROW * N_ROW + (r ^ (q % N_ROW)))


def ring_parts(own, along, split):
    before = permute(own, along(1))
    after = permute(own, along(-1))
    if not split:
        return [own, after, permute(before, along(1)), before]
    cut = own.shape[0] // 2
    return [own, after, permute(before[:cut], along(1)), permute(after[cut:], along(-1)), before]


def plane_gather(first, second):
    one = jnp.stack(ring_parts(first, along_x, False))
    two = jnp.stack(ring_parts(second, along_y, False))
    return ring_parts(one, along_y, True), ring_parts(two, along_x, True)


def dot(left, right):
    return jnp.dot(left, right, preferred_element_type=jnp.float32)


def dot_nt(left, right):
    return lax.dot_general(left, right, (((1,), (1,)), ((), ())), preferred_element_type=jnp.float32)


def cat(parts, axis):
    return jnp.concatenate(parts, axis)


def load(pairs, sems):
    copies = [pltpu.make_async_copy(src, dst, sems.at[i]) for i, (src, dst) in enumerate(pairs)]
    for copy in copies:
        copy.start()
    for copy in copies:
        copy.wait()


def spread(parts, held):
    at = 0
    pairs = []
    for part in parts:
        pairs.append((part, held.at[pl.ds(at, part.shape[0])]))
        at += part.shape[0]
    return pairs


def root_kernel(slot_one, slot_two, *refs):
    parts, (right_in, out_ref, one_ref, two_ref, right_ref, acc, sems) = refs[:10], refs[10:]
    load(spread(parts[:5], one_ref) + spread(parts[5:], two_ref) + [(right_in, right_ref)], sems)
    acc[...] = jnp.zeros_like(acc)

    def step(r, carry):
        right = [right_ref[r, pl.ds(BLK * i, BLK), :] for i in range(6)]
        right_0 = right[0]
        right_1 = cat(right[1:3], 1)
        right_2 = cat(right[3:6], 1)
        for side in range(2):
            one = slot_one[side * N_ROW + r]
            two = slot_two[side * N_ROW + r]
            acc[side] += dot(two_ref[two], right_2)
            acc[side, : 2 * BLK, : 2 * BLK] += dot(one_ref[one, BLK:, :], right_1)
            acc[side, :BLK, :BLK] += dot(one_ref[one, :BLK, :], right_0)
        return carry

    lax.fori_loop(0, N_ROW, step, 0)
    for outer in range(3):
        for side in range(2):
            out_ref[pl.ds((2 * outer + side) * BLK, BLK), :] = acc[
                side, pl.ds(outer * BLK, BLK), :
            ].astype(out_ref.dtype)


def pick_kernel(mine_ref, other_ref, row_ref, col_ref, root_ref, picked_ref):
    total = mine_ref[...].astype(jnp.float32) + other_ref[...].astype(jnp.float32)
    root_ref[...] = total
    low = total.astype(jnp.bfloat16)
    lanes = lax.broadcasted_iota(jnp.int32, (REACH, BLK), 1)

    def chooser(ref, i):
        return jnp.where(ref[pl.ds(i * REACH, REACH), :] == lanes, 1.0, 0.0).astype(jnp.bfloat16)

    rows = cat(
        [dot(chooser(row_ref, i), low[i * BLK : (i + 1) * BLK, :]).astype(jnp.bfloat16) for i in range(6)], 0
    )
    for i in range(3):
        picked_ref[pl.ds(i * REACH, REACH), :] = dot_nt(
            chooser(col_ref, i), rows[:, i * BLK : (i + 1) * BLK]
        ).astype(jnp.bfloat16)


def offdiag_kernel(slot_one, slot_two, *refs):
    parts, (right_in, out_ref, low_ref, one_ref, two_ref, block_ref, acc, sems) = refs[:10], refs[10:]
    block_in = right_in.at[:, pl.ds(768, 768), :]
    load(spread(parts[:5], one_ref) + spread(parts[5:], two_ref) + [(block_in, block_ref)], sems)
    acc[...] = jnp.zeros_like(acc)

    def step(r, carry):
        left = cat([block_ref[r, pl.ds(256 * i, 256), :] for i in range(3)], 1)
        right = cat(
            [
                one_ref[slot_one[r]],
                two_ref[slot_two[r]],
                one_ref[slot_one[N_ROW + r]],
                two_ref[slot_two[N_ROW + r]],
            ],
            0,
        )
        acc[...] += dot(left, right)
        return carry

    lax.fori_loop(0, N_ROW, step, 0)
    total = -acc[...]
    low_ref[...] = total.astype(low_ref.dtype)
    out_ref[...] = total.T


def own_kernel(slots, left_in, right_in, out_ref, left_ref, right_ref, acc, sems):
    first = pl.ds(0, 768)
    load([(left_in.at[:, first, :], left_ref), (right_in.at[:, first, :], right_ref)], sems)
    acc[...] = jnp.zeros_like(acc)

    def step(r, carry):
        right = [right_ref[r, pl.ds(BLK * i, BLK), :] for i in range(6)]
        right_0 = cat(right[0:2], 0)
        right_1 = cat([cat(right[2:4], 1), cat(right[4:6], 1)], 0)
        for side in range(2):
            slot = slots[side * N_ROW + r]
            left_0 = cat([left_ref[slot, :BLK, :], left_ref[slot, BLK : 2 * BLK, :]], 1)
            left_1 = cat([left_ref[slot, 2 * BLK : 4 * BLK, :], left_ref[slot, 4 * BLK : 6 * BLK, :]], 1)
            acc[side] += dot(left_1, right_1)
            acc[side, :BLK, :BLK] += dot(left_0, right_0)
        return carry

    lax.fori_loop(0, N_ROW, step, 0)
    out_ref[...] = acc[...]


def child_kernel(slots, part_slots, *refs):
    parts, (own_in, left_in, out_ref, left_ref, right_ref, acc, sems) = refs[:10], refs[10:]
    pairs = [(left_in.at[:, pl.ds(768, 768), :], left_ref), (own_in, acc)]
    at = 0
    for part in parts:
        pairs.append((part, right_ref.at[at // 256, pl.ds(at % 256, part.shape[0]), :]))
        at += part.shape[0]
    load(pairs, sems)

    def step(r, carry):
        right = right_ref[part_slots[r]]
        for side in range(2):
            slot = slots[side * N_ROW + r]
            left = cat([left_ref[slot, pl.ds(256 * i, 256), :] for i in range(3)], 1)
            acc[side] -= dot_nt(left, right)
        return carry

    lax.fori_loop(0, N_ROW, step, 0)
    for outer in range(2):
        for side in range(2):
            out_ref[pl.ds((2 * outer + side) * BLK, BLK), :] = acc[side, pl.ds(outer * BLK, BLK), :]


def call(kernel, scalars, arrays, outs, scratch, space=pl.ANY):
    vmem = pl.BlockSpec(memory_space=pltpu.VMEM)
    smem = pl.BlockSpec(memory_space=pltpu.SMEM)
    return pl.pallas_call(
        kernel,
        in_specs=[smem] * len(scalars) + [pl.BlockSpec(memory_space=space)] * len(arrays),
        out_specs=[vmem] * len(outs),
        out_shape=[jax.ShapeDtypeStruct(*o) for o in outs],
        scratch_shapes=list(scratch),
        compiler_params=pltpu.CompilerParams(vmem_limit_bytes=VMEM_LIMIT),
    )(*scalars, *arrays)


def stack_blocks(array, pairs):
    return jnp.concatenate([array[a, :, b, :] for a, b in pairs], 0)


def per_device(root_factor, root_pivots, child_factor, child_pivots, child_block, child_rows):
    row = lax.axis_index("row")
    col = lax.axis_index("col")
    bf16 = jnp.bfloat16
    root = root_factor.reshape(3, BLK, 3, BLK)
    scaled_root = (root_pivots.reshape(3, BLK, 1, 1) * root.astype(jnp.float32)).astype(bf16)
    root_pairs = [(0, 0), (1, 0), (1, 1), (2, 0), (2, 1), (2, 2)]
    root_turned = stack_blocks(root.transpose(0, 3, 2, 1), root_pairs)
    root_scaled = stack_blocks(scaled_root, root_pairs)

    child = child_factor.reshape(4, BLK, 2, BLK)
    scaled_child = (child_pivots.reshape(4, BLK, 1, 1) * child.astype(jnp.float32)).astype(bf16)
    child_pairs = [(0, 0), (1, 0), (2, 0), (2, 1), (3, 0), (3, 1)]
    child_turned = stack_blocks(child.transpose(0, 3, 2, 1), child_pairs)
    child_scaled = stack_blocks(scaled_child, child_pairs)
    block = child_block.reshape(6 * REACH, 2 * BLK)
    block_turned = block.T.reshape(2 * BLK, 3, BLK).transpose(1, 0, 2).reshape(768, BLK)
    block_sorted = block.reshape(3, 2, REACH, 2 * BLK).transpose(1, 0, 2, 3).reshape(6 * REACH, 2 * BLK)
    block_sorted = block_sorted.T.reshape(2 * BLK, 3, BLK).transpose(1, 0, 2).reshape(768, BLK)

    root_right = lax.all_gather(root_scaled, "row", axis=0, tiled=False)
    root_here = permute(root_turned, transposed_place)
    child_stack = jnp.concatenate([child_turned, block_turned], 0)
    root_here, child_stack = lax.optimization_barrier((root_here, child_stack))
    child_here = permute(child_stack, transposed_place)
    child_right = lax.all_gather(jnp.concatenate([child_scaled, block_sorted], 0), "row", axis=0, tiled=False)

    root_parts = plane_gather(root_here[:384], root_here[384:])
    child_here, root_parts = lax.optimization_barrier((child_here, root_parts))
    child_left = lax.all_gather(child_here, "col", axis=0, tiled=False)

    side = jnp.arange(2, dtype=jnp.int32)[:, None]
    classes = jnp.arange(N_ROW, dtype=jnp.int32)[None, :]
    source = side * N_ROW + (classes ^ row)
    my_x, my_y = col % SIDE, col // SIDE

    def plane_slots(place):
        dx = (place % SIDE - my_x) % SIDE
        dy = (place // SIDE - my_y) % SIDE
        return (dy * SIDE + dx).reshape(-1), (dx * SIDE + dy).reshape(-1)

    root_slots = plane_slots(source)
    (partial,) = call(
        root_kernel,
        root_slots,
        (*root_parts[0], *root_parts[1], root_right),
        [((768, 384), bf16)],
        [
            pltpu.VMEM((N_COL, 384, BLK), bf16),
            pltpu.VMEM((N_COL, 384, BLK), bf16),
            pltpu.VMEM((N_ROW, 768, BLK), bf16),
            pltpu.VMEM((2, 384, 384), jnp.float32),
            pltpu.SemaphoreType.DMA((11,)),
        ],
    )
    other = permute(partial, other_half)
    rows = child_rows[0].reshape(48, REACH) % BLK
    row_picks = lax.dynamic_index_in_dim(rows.reshape(6, N_ROW, REACH), row, 1, keepdims=False)
    col_picks = lax.dynamic_index_in_dim(rows.reshape(3, N_COL, REACH), col, 1, keepdims=False)
    root_inverse, picked = call(
        pick_kernel,
        (),
        (partial, other, row_picks.reshape(-1, 1), col_picks.reshape(-1, 1)),
        [((768, 384), jnp.float32), ((192, 384), bf16)],
        (),
        pltpu.VMEM,
    )
    picked_parts = plane_gather(picked[:96], picked[96:])
    offdiag_slots = plane_slots(side * N_ROW + classes)
    offdiag, offdiag_low = call(
        offdiag_kernel,
        offdiag_slots,
        (*picked_parts[0], *picked_parts[1], child_right),
        [((384, 256), jnp.float32), ((256, 384), bf16)],
        [
            pltpu.VMEM((N_COL, 96, 384), bf16),
            pltpu.VMEM((N_COL, 96, 384), bf16),
            pltpu.VMEM((N_ROW, 768, BLK), bf16),
            pltpu.VMEM((256, 384), jnp.float32),
            pltpu.SemaphoreType.DMA((11,)),
        ],
    )
    slots = source.reshape(-1)
    (own,) = call(
        own_kernel,
        (slots,),
        (child_left, child_right),
        [((2, 256, 256), jnp.float32)],
        [
            pltpu.VMEM((N_COL, 768, BLK), bf16),
            pltpu.VMEM((N_ROW, 768, BLK), bf16),
            pltpu.VMEM((2, 256, 256), jnp.float32),
            pltpu.SemaphoreType.DMA((2,)),
        ],
    )
    line = ring_parts(offdiag_low, along_z, True)
    parts = line + [permute(part, other_core) for part in line]
    r = classes[0]
    part_slots = ((r ^ row) & 1) * SIDE + (r // 2 - row // 2) % SIDE
    (child_inverse,) = call(
        child_kernel,
        (slots, part_slots),
        (*parts, own, child_left),
        [((512, 256), jnp.float32)],
        [
            pltpu.VMEM((N_COL, 768, BLK), bf16),
            pltpu.VMEM((N_ROW, 256, 384), bf16),
            pltpu.VMEM((2, 256, 256), jnp.float32),
            pltpu.SemaphoreType.DMA((12,)),
        ],
    )
    return (
        root_inverse.reshape(6, 1, BLK, 3, 1, BLK),
        offdiag.reshape(child_block.shape),
        child_inverse.reshape(child_factor.shape),
    )


def solution(mesh):
    return jax.shard_map(
        per_device,
        mesh=mesh,
        in_specs=(
            P(None, ("half", "row"), None, None, "col", None),
            P(None, ("half", "row"), None),
            P("half", None, "row", None, None, "col", None),
            P("half", None, "row", None),
            P("half", None, "row", None, None, "col", None),
            P("half", None),
        ),
        out_specs=(
            P(None, "row", None, None, "col", None),
            P("half", None, "row", None, None, "col", None),
            P("half", None, "row", None, None, "col", None),
        ),
        check_vma=False,
    )
```

```python
import functools

import jax
import jax.numpy as jnp
from jax import lax
from jax.experimental import pallas as pl
from jax.experimental.pallas import tpu as pltpu
from jax.sharding import PartitionSpec as P

AXES = ("half", "row", "col")
N_HALF, N_ROW, N_COL = 2, 8, 16
SIDE = 4
BLK = 128
REACH = 64
VMEM_LIMIT = 60 * 1024 * 1024


def permute(array, target):
    pairs = []
    for half in range(N_HALF):
        for row in range(N_ROW):
            for col in range(N_COL):
                to_half, to_row, to_col = target(half, row, col)
                pairs.append(
                    (
                        (half * N_ROW + row) * N_COL + col,
                        (to_half * N_ROW + to_row) * N_COL + to_col,
                    )
                )
    return lax.ppermute(array, AXES, pairs)


def along_x(step):
    return lambda h, r, q: (h, r, q // SIDE * SIDE + (q + step) % SIDE)


def along_y(step):
    return lambda h, r, q: (h, r, (q + SIDE * step) % N_COL)


def along_z(step):
    return lambda h, r, q: (h, (r + 2 * step) % N_ROW, q)


def other_core(h, r, q):
    return (h, r ^ 1, q)


def other_half(h, r, q):
    return (1 - h, r, q)


def mixed(r, p):
    return r ^ p ^ (r % 2 * SIDE)


def transposed_place(h, r, q):
    return (h, q % N_ROW, q // N_ROW * N_ROW + mixed(r, q % N_ROW))


def ring_parts(own, along, split):
    before = permute(own, along(1))
    after = permute(own, along(-1))
    if not split:
        return [own, after, permute(before, along(1)), before]
    cut = own.shape[0] // 2
    return [own, after, permute(before[:cut], along(1)), permute(after[cut:], along(-1)), before]


def plane_gather(first, second):
    one = jnp.stack(ring_parts(first, along_x, False))
    two = jnp.stack(ring_parts(second, along_y, False))
    return ring_parts(one, along_y, True), ring_parts(two, along_x, True)


def dot(left, right):
    return jnp.dot(left, right, preferred_element_type=jnp.float32)


def dot_nt(left, right):
    return lax.dot_general(left, right, (((1,), (1,)), ((), ())), preferred_element_type=jnp.float32)


def cat(parts, axis):
    return jnp.concatenate(parts, axis)


def load(pairs, sems):
    copies = [pltpu.make_async_copy(src, dst, sems.at[i]) for i, (src, dst) in enumerate(pairs)]
    for copy in copies:
        copy.start()
    for copy in copies:
        copy.wait()


def spread(parts, held):
    at = 0
    pairs = []
    for part in parts:
        pairs.append((part, held.at[pl.ds(at, part.shape[0])]))
        at += part.shape[0]
    return pairs


def chooser(ref, i):
    lanes = lax.broadcasted_iota(jnp.int32, (REACH, BLK), 1)
    return jnp.where(ref[pl.ds(i * REACH, REACH), :] == lanes, 1.0, 0.0).astype(jnp.bfloat16)


def pick(low_ref, row_ref, col_ref, picked_ref):
    rows = cat(
        [dot(chooser(row_ref, i), low_ref[pl.ds(i * BLK, BLK), :]).astype(jnp.bfloat16) for i in range(6)], 0
    )
    for i in range(3):
        picked_ref[pl.ds(i * REACH, REACH), :] = dot_nt(
            chooser(col_ref, i), rows[:, i * BLK : (i + 1) * BLK]
        ).astype(jnp.bfloat16)


def root_kernel(slot_one, slot_two, *refs):
    parts, right_in, picks = refs[:10], refs[10], refs[11:15]
    out_ref, theirs_ref, mine_ref, one_ref, two_ref, right_ref, acc, sems = refs[15:]
    right_in = right_in.at[:, pl.ds(0, 768), :]
    load(spread(parts[:5], one_ref) + spread(parts[5:], two_ref) + [(right_in, right_ref)], sems)
    acc[...] = jnp.zeros_like(acc)

    def step(i, carry):
        pair = (2 * i, 2 * i + 1)
        right = [[right_ref[r, pl.ds(BLK * k, BLK), :] for k in range(6)] for r in pair]
        right_0 = cat([right[0][0], right[1][0]], 0)
        right_1 = cat([cat(right[k][1:3], 1) for k in range(2)], 0)
        right_2 = cat([cat(right[k][3:6], 1) for k in range(2)], 0)
        for side in range(2):
            one = [slot_one[side * N_ROW + r] for r in pair]
            two = [slot_two[side * N_ROW + r] for r in pair]
            left_1 = cat([one_ref[one[k]] for k in range(2)], 1)
            left_2 = cat([two_ref[two[k]] for k in range(2)], 1)
            acc[side] += dot(left_2, right_2)
            acc[side, : 2 * BLK, : 2 * BLK] += dot(left_1[BLK:], right_1)
            acc[side, :BLK, :BLK] += dot(left_1[:BLK], right_0)
        return carry

    lax.fori_loop(0, N_ROW // 2, step, 0)
    for outer in range(3):
        for side in range(2):
            out_ref[pl.ds((2 * outer + side) * BLK, BLK), :] = acc[
                side, pl.ds(outer * BLK, BLK), :
            ].astype(out_ref.dtype)
    pick(out_ref, picks[0], picks[1], theirs_ref)
    pick(out_ref, picks[2], picks[3], mine_ref)


def sum_kernel(mine_ref, other_ref, out_ref):
    for i in range(3):
        lanes = pl.ds(i * BLK, BLK)
        out_ref[pl.ds(i, 768, stride=3), :] = mine_ref[:, lanes].astype(jnp.float32) + other_ref[
            :, lanes
        ].astype(jnp.float32)


def offdiag_kernel(slot_one, slot_two, *refs):
    parts, (right_in, out_ref, low_ref, one_ref, two_ref, block_ref, acc, sems) = refs[:10], refs[10:]
    block_in = right_in.at[:, pl.ds(1536, 768), :]
    load(spread(parts[:5], one_ref) + spread(parts[5:], two_ref) + [(block_in, block_ref)], sems)
    acc[...] = jnp.zeros_like(acc)

    def step(r, carry):
        left = cat([block_ref[r, pl.ds(256 * i, 256), :] for i in range(3)], 1)
        right = cat(
            [
                one_ref[slot_one[r]],
                two_ref[slot_two[r]],
                one_ref[slot_one[N_ROW + r]],
                two_ref[slot_two[N_ROW + r]],
            ],
            0,
        )
        acc[...] += dot(left, right)
        return carry

    lax.fori_loop(0, N_ROW, step, 0)
    total = -acc[...]
    low_ref[...] = total.astype(low_ref.dtype)
    for i in range(2):
        out_ref[pl.ds(i, 384, stride=2), :] = total[i * BLK : (i + 1) * BLK, :].T


def own_kernel(slots, left_in, right_in, out_ref, left_ref, right_ref, acc, sems):
    left_in = left_in.at[:, pl.ds(0, 768), :]
    right_in = right_in.at[:, pl.ds(768, 768), :]
    load([(left_in, left_ref), (right_in, right_ref)], sems)
    acc[...] = jnp.zeros_like(acc)

    def step(r, carry):
        right = [right_ref[r, pl.ds(BLK * i, BLK), :] for i in range(6)]
        right_0 = cat(right[0:2], 0)
        right_1 = cat([cat(right[2:4], 1), cat(right[4:6], 1)], 0)
        for side in range(2):
            slot = slots[side * N_ROW + r]
            left_0 = cat([left_ref[slot, :BLK, :], left_ref[slot, BLK : 2 * BLK, :]], 1)
            left_1 = cat([left_ref[slot, 2 * BLK : 4 * BLK, :], left_ref[slot, 4 * BLK : 6 * BLK, :]], 1)
            acc[side] += dot(left_1, right_1)
            acc[side, :BLK, :BLK] += dot(left_0, right_0)
        return carry

    lax.fori_loop(0, N_ROW, step, 0)
    out_ref[...] = acc[...]


def child_kernel(slots, part_slots, *refs):
    parts, (own_in, left_in, out_ref, left_ref, right_ref, acc, sems) = refs[:10], refs[10:]
    pairs = [(left_in.at[:, pl.ds(768, 768), :], left_ref), (own_in, acc)]
    at = 0
    for part in parts:
        pairs.append((part, right_ref.at[at // 256, pl.ds(at % 256, part.shape[0]), :]))
        at += part.shape[0]
    load(pairs, sems)

    def step(i, carry):
        pair = (2 * i, 2 * i + 1)
        right = cat([right_ref[part_slots[r]] for r in pair], 1)
        for side in range(2):
            held = [slots[side * N_ROW + r] for r in pair]
            left = cat([left_ref[slot, pl.ds(256 * k, 256), :] for slot in held for k in range(3)], 1)
            acc[side] -= dot_nt(left, right)
        return carry

    lax.fori_loop(0, N_ROW // 2, step, 0)
    for outer in range(2):
        for side in range(2):
            for i in range(2):
                first = (2 * outer + side) * 2 * BLK + i
                out_ref[pl.ds(first, BLK, stride=2), :] = acc[
                    side, pl.ds(outer * BLK, BLK), pl.ds(i * BLK, BLK)
                ]


def call(kernel, scalars, arrays, outs, scratch, blocks=()):
    vmem = pl.BlockSpec(memory_space=pltpu.VMEM)
    smem = pl.BlockSpec(memory_space=pltpu.SMEM)
    anywhere = pl.BlockSpec(memory_space=pl.ANY)
    return pl.pallas_call(
        kernel,
        in_specs=[smem] * len(scalars) + [anywhere] * len(arrays) + [vmem] * len(blocks),
        out_specs=[vmem] * len(outs),
        out_shape=[jax.ShapeDtypeStruct(*o) for o in outs],
        scratch_shapes=list(scratch),
        compiler_params=pltpu.CompilerParams(vmem_limit_bytes=VMEM_LIMIT),
    )(*scalars, *arrays, *blocks)


def stack_blocks(array, pairs):
    return jnp.concatenate([array[a, :, b, :] for a, b in pairs], 0)


def per_device(root_factor, root_pivots, child_factor, child_pivots, child_block, child_rows):
    row = lax.axis_index("row")
    col = lax.axis_index("col")
    bf16 = jnp.bfloat16
    root = root_factor.reshape(3, BLK, 3, BLK)
    root_pairs = [(0, 0), (1, 0), (1, 1), (2, 0), (2, 1), (2, 2)]
    root_here = permute(stack_blocks(root.transpose(0, 3, 2, 1), root_pairs), transposed_place)
    scaled_root = (root_pivots.reshape(3, BLK, 1, 1) * root.astype(jnp.float32)).astype(bf16)
    root_scaled = stack_blocks(scaled_root, root_pairs)

    child = child_factor.reshape(4, BLK, 2, BLK)
    scaled_child = (child_pivots.reshape(4, BLK, 1, 1) * child.astype(jnp.float32)).astype(bf16)
    child_pairs = [(0, 0), (1, 0), (2, 0), (2, 1), (3, 0), (3, 1)]
    child_turned = stack_blocks(child.transpose(0, 3, 2, 1), child_pairs)
    child_scaled = stack_blocks(scaled_child, child_pairs)
    block = child_block.reshape(6 * REACH, 2 * BLK)
    block_turned = block.T.reshape(2 * BLK, 3, BLK).transpose(1, 0, 2).reshape(768, BLK)
    block_sorted = block.reshape(3, 2, REACH, 2 * BLK).transpose(1, 0, 2, 3).reshape(6 * REACH, 2 * BLK)
    block_sorted = block_sorted.T.reshape(2 * BLK, 3, BLK).transpose(1, 0, 2).reshape(768, BLK)
    right = lax.all_gather(
        jnp.concatenate([root_scaled, child_scaled, block_sorted], 0), "row", axis=0, tiled=False
    )

    rows = child_rows[0].reshape(48, REACH) % BLK
    row_picks = lax.dynamic_index_in_dim(rows.reshape(6, N_ROW, REACH), row, 1, keepdims=False)
    col_picks = lax.dynamic_index_in_dim(rows.reshape(3, N_COL, REACH), col, 1, keepdims=False)
    my_picks = jnp.concatenate([row_picks.reshape(-1), col_picks.reshape(-1)])[:, None]
    other_picks = permute(my_picks, other_half)

    child_stack = jnp.concatenate([child_turned, block_turned], 0)
    child_stack = lax.optimization_barrier((child_stack, root_here))[0]
    child_here = permute(child_stack, transposed_place)
    root_parts = plane_gather(root_here[:384], root_here[384:])
    child_here = lax.optimization_barrier((child_here, root_parts))[0]
    child_left = lax.all_gather(child_here, "col", axis=0, tiled=False)

    side = jnp.arange(2, dtype=jnp.int32)[:, None]
    classes = jnp.arange(N_ROW, dtype=jnp.int32)[None, :]
    source = side * N_ROW + mixed(classes, row)
    my_x, my_y = col % SIDE, col // SIDE

    def plane_slots(place):
        dx = (place % SIDE - my_x) % SIDE
        dy = (place // SIDE - my_y) % SIDE
        return (dy * SIDE + dx).reshape(-1), (dx * SIDE + dy).reshape(-1)

    root_slots = plane_slots(source)
    partial, theirs, mine = call(
        root_kernel,
        root_slots,
        (*root_parts[0], *root_parts[1], right),
        [((768, 384), bf16), ((192, 384), bf16), ((192, 384), bf16)],
        [
            pltpu.VMEM((N_COL, 384, BLK), bf16),
            pltpu.VMEM((N_COL, 384, BLK), bf16),
            pltpu.VMEM((N_ROW, 768, BLK), bf16),
            pltpu.VMEM((2, 384, 384), jnp.float32),
            pltpu.SemaphoreType.DMA((11,)),
        ],
        (other_picks[:384], other_picks[384:], my_picks[:384], my_picks[384:]),
    )
    theirs = permute(theirs, other_half)
    picked = (mine.astype(jnp.float32) + theirs.astype(jnp.float32)).astype(bf16)
    late = lax.optimization_barrier((partial, picked))[0]
    (root_inverse,) = call(
        sum_kernel, (), (), [((2304, BLK), jnp.float32)], (), (partial, permute(late, other_half))
    )
    picked_parts = plane_gather(picked[:96], picked[96:])
    offdiag_slots = plane_slots(side * N_ROW + classes)
    offdiag, offdiag_low = call(
        offdiag_kernel,
        offdiag_slots,
        (*picked_parts[0], *picked_parts[1], right),
        [((768, BLK), jnp.float32), ((256, 384), bf16)],
        [
            pltpu.VMEM((N_COL, 96, 384), bf16),
            pltpu.VMEM((N_COL, 96, 384), bf16),
            pltpu.VMEM((N_ROW, 768, BLK), bf16),
            pltpu.VMEM((256, 384), jnp.float32),
            pltpu.SemaphoreType.DMA((11,)),
        ],
    )
    slots = source.reshape(-1)
    (own,) = call(
        own_kernel,
        (slots,),
        (child_left, right),
        [((2, 256, 256), jnp.float32)],
        [
            pltpu.VMEM((N_COL, 768, BLK), bf16),
            pltpu.VMEM((N_ROW, 768, BLK), bf16),
            pltpu.VMEM((2, 256, 256), jnp.float32),
            pltpu.SemaphoreType.DMA((2,)),
        ],
    )
    line = ring_parts(offdiag_low, along_z, True)
    parts = line + [permute(part, other_core) for part in line]
    r = classes[0]
    part_slots = ((r ^ row) & 1) * SIDE + (r // 2 - row // 2) % SIDE
    (child_inverse,) = call(
        child_kernel,
        (slots, part_slots),
        (*parts, own, child_left),
        [((1024, BLK), jnp.float32)],
        [
            pltpu.VMEM((N_COL, 768, BLK), bf16),
            pltpu.VMEM((N_ROW, 256, 384), bf16),
            pltpu.VMEM((2, 256, 256), jnp.float32),
            pltpu.SemaphoreType.DMA((12,)),
        ],
    )
    return (
        root_inverse.reshape(6, 1, BLK, 3, 1, BLK),
        offdiag.reshape(child_block.shape),
        child_inverse.reshape(child_factor.shape),
    )


def solution(mesh):
    return jax.shard_map(
        per_device,
        mesh=mesh,
        in_specs=(
            P(None, ("half", "row"), None, None, "col", None),
            P(None, ("half", "row"), None),
            P("half", None, "row", None, None, "col", None),
            P("half", None, "row", None),
            P("half", None, "row", None, None, "col", None),
            P("half", None),
        ),
        out_specs=(
            P(None, "row", None, None, "col", None),
            P("half", None, "row", None, None, "col", None),
            P("half", None, "row", None, None, "col", None),
        ),
        check_vma=False,
    )
```

```python
import functools

import jax
import jax.numpy as jnp
from jax import lax
from jax.experimental import pallas as pl
from jax.experimental.pallas import tpu as pltpu
from jax.sharding import PartitionSpec as P

AXES = ("half", "row", "col")
N_HALF, N_ROW, N_COL = 2, 8, 16
SIDE = 4
BLK = 128
REACH = 64
ROOT_PAIRS = [(0, 0), (1, 0), (1, 1), (2, 0), (2, 1), (2, 2)]
CHILD_PAIRS = [(0, 0), (1, 0), (2, 0), (2, 1), (3, 0), (3, 1)]
VMEM_LIMIT = 60 * 1024 * 1024


def permute(array, target):
    pairs = []
    for half in range(N_HALF):
        for row in range(N_ROW):
            for col in range(N_COL):
                to_half, to_row, to_col = target(half, row, col)
                pairs.append(
                    (
                        (half * N_ROW + row) * N_COL + col,
                        (to_half * N_ROW + to_row) * N_COL + to_col,
                    )
                )
    return lax.ppermute(array, AXES, pairs)


def along_x(step):
    return lambda h, r, q: (h, r, q // SIDE * SIDE + (q + step) % SIDE)


def along_y(step):
    return lambda h, r, q: (h, r, (q + SIDE * step) % N_COL)


def along_z(step):
    return lambda h, r, q: (h, (r + 2 * step) % N_ROW, q)


def other_core(h, r, q):
    return (h, r ^ 1, q)


def other_half(h, r, q):
    return (1 - h, r, q)


def mixed(r, p):
    return (r // 2 - p // 2) % SIDE * 2 + (r ^ p) % 2


def transposed_place(h, r, q):
    return (h, q % N_ROW, q // N_ROW * N_ROW + mixed(r, q % N_ROW))


def ring_parts(own, along, split):
    before = permute(own, along(1))
    after = permute(own, along(-1))
    if not split:
        return [own, after, permute(before, along(1)), before]
    cut = own.shape[0] // 2
    return [own, after, permute(before[:cut], along(1)), permute(after[cut:], along(-1)), before]


def plane_gather(first, second):
    one = jnp.stack(ring_parts(first, along_x, False))
    two = jnp.stack(ring_parts(second, along_y, False))
    return ring_parts(one, along_y, True), ring_parts(two, along_x, True)


def dot(left, right):
    return jnp.dot(left, right, preferred_element_type=jnp.float32)


def dot_nt(left, right):
    return lax.dot_general(left, right, (((1,), (1,)), ((), ())), preferred_element_type=jnp.float32)


def cat(parts, axis):
    return jnp.concatenate(parts, axis)


def load(pairs, sems):
    copies = [pltpu.make_async_copy(src, dst, sems.at[i]) for i, (src, dst) in enumerate(pairs)]
    for copy in copies:
        copy.start()
    for copy in copies:
        copy.wait()


def spread(parts, held):
    at = 0
    pairs = []
    for part in parts:
        pairs.append((part, held.at[pl.ds(at, part.shape[0])]))
        at += part.shape[0]
    return pairs


def chooser(ref, i):
    lanes = lax.broadcasted_iota(jnp.int32, (REACH, BLK), 1)
    return jnp.where(ref[pl.ds(i * REACH, REACH), :] == lanes, 1.0, 0.0).astype(jnp.bfloat16)


def pick(low_ref, ref, picked_ref):
    rows = cat(
        [dot(chooser(ref, i), low_ref[pl.ds(i * BLK, BLK), :]).astype(jnp.bfloat16) for i in range(6)], 0
    )
    for i in range(3):
        picked_ref[pl.ds(i * REACH, REACH), :] = dot_nt(
            chooser(ref, 6 + i), rows[:, i * BLK : (i + 1) * BLK]
        ).astype(jnp.bfloat16)


def lines(parts, held):
    size = held.shape[1]
    at = 0
    pairs = []
    for part in parts:
        pairs.append((part, held.at[at // size, pl.ds(at % size, part.shape[0]), :]))
        at += part.shape[0]
    return pairs


def prepare_kernel(shared, *refs):
    root_ref, root_scale, child_ref, child_scale, block_ref = refs[:5]
    turned_refs, right_refs = (refs[5:7], refs[7:]) if shared == 1 else (refs[5:6] * 2, refs[6:])
    if len(right_refs) == 1:
        right_refs = right_refs * 2
    turned_base = 0 if shared == 1 else 768
    right_base = 768 if shared == 1 else 0

    def tile(ref, i, j):
        return ref[pl.ds(i * BLK, BLK), pl.ds(j * BLK, BLK)]

    def factor(ref, scale_ref, pairs, turned, right, turned_at, right_at):
        for i, (a, b) in enumerate(pairs):
            scale = jnp.broadcast_to(scale_ref[pl.ds(a, 1), :], (BLK, BLK)).T
            own = tile(ref, a, b)
            turned[pl.ds(turned_at + i * BLK, BLK), :] = own.T
            right[pl.ds(right_at + i * BLK, BLK), :] = (scale * own.astype(jnp.float32)).astype(
                jnp.bfloat16
            )

    factor(root_ref, root_scale, ROOT_PAIRS, turned_refs[0], right_refs[0], 0, 0)
    factor(child_ref, child_scale, CHILD_PAIRS, turned_refs[1], right_refs[1], turned_base, right_base)
    sort = [block_ref[pl.ds(REACH * a, REACH), :] for a in (0, 2, 4, 1, 3, 5)]
    for j in range(3):
        pair = cat(sort[2 * j : 2 * j + 2], 0)
        for i in range(2):
            at = 768 + j * 2 * BLK + i * BLK
            turned_refs[1][pl.ds(turned_base + at, BLK), :] = tile(block_ref, j, i).T
            right_refs[1][pl.ds(right_base + at, BLK), :] = pair[:, i * BLK : (i + 1) * BLK].T


def root_kernel(slot_one, slot_two, part_slots, *refs):
    parts, right_in, other_picks, my_picks = refs[:10], refs[10:20], refs[20], refs[21]
    out_ref, theirs_ref, mine_ref, one_ref, two_ref, right_ref, acc, sems = refs[22:]
    load(spread(parts[:5], one_ref) + spread(parts[5:], two_ref) + lines(right_in, right_ref), sems)
    acc[...] = jnp.zeros_like(acc)

    def step(i):
        pair = (2 * i, 2 * i + 1)
        right = [[right_ref[part_slots[r], pl.ds(BLK * k, BLK), :] for k in range(6)] for r in pair]
        right_0 = cat([right[0][0], right[1][0]], 0)
        right_1 = cat([cat(right[k][1:3], 1) for k in range(2)], 0)
        right_2 = cat([cat(right[k][3:6], 1) for k in range(2)], 0)
        for side in range(2):
            one = [slot_one[side * N_ROW + r] for r in pair]
            two = [slot_two[side * N_ROW + r] for r in pair]
            left_1 = cat([one_ref[one[k]] for k in range(2)], 1)
            left_2 = cat([two_ref[two[k]] for k in range(2)], 1)
            acc[side] += dot(left_2, right_2)
            acc[side, : 2 * BLK, : 2 * BLK] += dot(left_1[BLK:], right_1)
            acc[side, :BLK, :BLK] += dot(left_1[:BLK], right_0)

    for i in range(N_ROW // 2):
        step(i)
    for outer in range(3):
        for side in range(2):
            out_ref[pl.ds((2 * outer + side) * BLK, BLK), :] = acc[
                side, pl.ds(outer * BLK, BLK), :
            ].astype(out_ref.dtype)
    pick(out_ref, other_picks, theirs_ref)
    pick(out_ref, my_picks, mine_ref)


def sum_kernel(mine_ref, other_ref, out_ref):
    for i in range(3):
        lanes = pl.ds(i * BLK, BLK)
        out_ref[pl.ds(i, 768, stride=3), :] = mine_ref[:, lanes].astype(jnp.float32) + other_ref[
            :, lanes
        ].astype(jnp.float32)


def offdiag_kernel(slot_one, slot_two, *refs):
    parts, (right_in, out_ref, low_ref, one_ref, two_ref, block_ref, acc, sems) = refs[:10], refs[10:]
    block_in = right_in.at[:, pl.ds(768, 768), :]
    load(spread(parts[:5], one_ref) + spread(parts[5:], two_ref) + [(block_in, block_ref)], sems)
    acc[...] = jnp.zeros_like(acc)

    def step(r):
        left = cat([block_ref[r, pl.ds(256 * i, 256), :] for i in range(3)], 1)
        right = cat(
            [
                one_ref[slot_one[r]],
                two_ref[slot_two[r]],
                one_ref[slot_one[N_ROW + r]],
                two_ref[slot_two[N_ROW + r]],
            ],
            0,
        )
        acc[...] += dot(left, right)

    for i in range(N_ROW):
        step(i)
    total = -acc[...]
    low_ref[...] = total.astype(low_ref.dtype)
    for i in range(2):
        out_ref[pl.ds(i, 384, stride=2), :] = total[i * BLK : (i + 1) * BLK, :].T


def child_kernel(slots, part_slots, *refs):
    parts, (left_in, right_in, out_ref, left_ref, factor_ref, right_ref, acc, sems) = refs[:10], refs[10:]
    first, second = pl.ds(0, 768), pl.ds(768, 768)
    pairs = [
        (left_in.at[:, first, :], left_ref.at[:, first, :]),
        (right_in.at[:, pl.ds(0, 768), :], factor_ref),
        (left_in.at[:, second, :], left_ref.at[:, second, :]),
    ]
    at = 0
    for part in parts:
        pairs.append((part, right_ref.at[at // 256, pl.ds(at % 256, part.shape[0]), :]))
        at += part.shape[0]
    copies = [pltpu.make_async_copy(src, dst, sems.at[i]) for i, (src, dst) in enumerate(pairs)]
    for copy in copies:
        copy.start()
    acc[...] = jnp.zeros_like(acc)
    for copy in copies[:2]:
        copy.wait()

    def own(r):
        right = [factor_ref[r, pl.ds(BLK * i, BLK), :] for i in range(6)]
        right_0 = cat(right[0:2], 0)
        right_1 = cat([cat(right[2:4], 1), cat(right[4:6], 1)], 0)
        for side in range(2):
            slot = slots[side * N_ROW + r]
            left_0 = cat([left_ref[slot, :BLK, :], left_ref[slot, BLK : 2 * BLK, :]], 1)
            left_1 = cat([left_ref[slot, 2 * BLK : 4 * BLK, :], left_ref[slot, 4 * BLK : 6 * BLK, :]], 1)
            acc[side] += dot(left_1, right_1)
            acc[side, :BLK, :BLK] += dot(left_0, right_0)

    for r in range(N_ROW):
        own(r)
    for copy in copies[2:]:
        copy.wait()

    def coupled(i):
        pair = (2 * i, 2 * i + 1)
        right = cat([right_ref[part_slots[r]] for r in pair], 1)
        for side in range(2):
            held = [slots[side * N_ROW + r] for r in pair]
            left = cat([left_ref[slot, pl.ds(768 + 256 * k, 256), :] for slot in held for k in range(3)], 1)
            acc[side] -= dot_nt(left, right)

    for i in range(N_ROW // 2):
        coupled(i)
    for outer in range(2):
        for side in range(2):
            for i in range(2):
                at = (2 * outer + side) * 2 * BLK + i
                out_ref[pl.ds(at, BLK, stride=2), :] = acc[
                    side, pl.ds(outer * BLK, BLK), pl.ds(i * BLK, BLK)
                ]


def call(kernel, scalars, arrays, outs, scratch, blocks=()):
    vmem = pl.BlockSpec(memory_space=pltpu.VMEM)
    smem = pl.BlockSpec(memory_space=pltpu.SMEM)
    anywhere = pl.BlockSpec(memory_space=pl.ANY)
    return pl.pallas_call(
        kernel,
        in_specs=[smem] * len(scalars) + [anywhere] * len(arrays) + [vmem] * len(blocks),
        out_specs=[vmem] * len(outs),
        out_shape=[jax.ShapeDtypeStruct(*o) for o in outs],
        scratch_shapes=list(scratch),
        compiler_params=pltpu.CompilerParams(vmem_limit_bytes=VMEM_LIMIT),
    )(*scalars, *arrays, *blocks)


def per_device(root_factor, root_pivots, child_factor, child_pivots, child_block, child_rows):
    row = lax.axis_index("row")
    col = lax.axis_index("col")
    bf16 = jnp.bfloat16
    all_turned, root_scaled, child_right = call(
        functools.partial(prepare_kernel, 2),
        (),
        (),
        [((2304, BLK), bf16), ((768, BLK), bf16), ((1536, BLK), bf16)],
        (),
        (
            root_factor.reshape(384, 384),
            root_pivots.reshape(3, BLK),
            child_factor.reshape(512, 256),
            child_pivots.reshape(4, BLK),
            child_block.reshape(384, 256),
        ),
    )
    turned = permute(all_turned, transposed_place)
    root_line = ring_parts(root_scaled, along_z, True)
    root_right = root_line + [permute(part, other_core) for part in root_line]
    rows = child_rows[0].reshape(48, REACH) % BLK
    row_picks = lax.dynamic_index_in_dim(rows.reshape(6, N_ROW, REACH), row, 1, keepdims=False)
    col_picks = lax.dynamic_index_in_dim(rows.reshape(3, N_COL, REACH), col, 1, keepdims=False)
    my_picks = jnp.concatenate([row_picks.reshape(-1), col_picks.reshape(-1)])[:, None]
    other_picks = permute(my_picks, other_half)

    side = jnp.arange(2, dtype=jnp.int32)[:, None]
    classes = jnp.arange(N_ROW, dtype=jnp.int32)[None, :]
    source = side * N_ROW + mixed(classes, row)
    my_x, my_y = col % SIDE, col // SIDE

    def plane_slots(place):
        dx = (place % SIDE - my_x) % SIDE
        dy = (place // SIDE - my_y) % SIDE
        return (dy * SIDE + dx).reshape(-1), (dx * SIDE + dy).reshape(-1)

    root_slots = plane_slots(source)
    offdiag_slots = plane_slots(side * N_ROW + classes)
    slots = source.reshape(-1)
    r = classes[0]
    part_slots = ((r ^ row) & 1) * SIDE + (r // 2 - row // 2) % SIDE
    turned, root_right, root_slots, offdiag_slots, slots, part_slots, my_picks, other_picks = (
        lax.optimization_barrier(
            (turned, root_right, root_slots, offdiag_slots, slots, part_slots, my_picks, other_picks)
        )
    )
    child_right = lax.optimization_barrier((child_right, turned))[0]
    right = lax.all_gather(child_right, "row", axis=0, tiled=False)
    root_parts = plane_gather(turned[:384], turned[384:768])

    partial, theirs, mine = call(
        root_kernel,
        (*root_slots, part_slots),
        (*root_parts[0], *root_parts[1], *root_right),
        [((768, 384), bf16), ((192, 384), bf16), ((192, 384), bf16)],
        [
            pltpu.VMEM((N_COL, 384, BLK), bf16),
            pltpu.VMEM((N_COL, 384, BLK), bf16),
            pltpu.VMEM((N_ROW, 768, BLK), bf16),
            pltpu.VMEM((2, 384, 384), jnp.float32),
            pltpu.SemaphoreType.DMA((20,)),
        ],
        (other_picks, my_picks),
    )
    theirs = permute(theirs, other_half)
    child_here = lax.optimization_barrier((turned[768:], root_parts))[0]
    child_left = lax.all_gather(child_here, "col", axis=0, tiled=False)
    picked = (mine.astype(jnp.float32) + theirs.astype(jnp.float32)).astype(bf16)
    late = lax.optimization_barrier((partial, picked))[0]
    late = permute(late, other_half)
    (root_inverse,) = call(sum_kernel, (), (), [((2304, BLK), jnp.float32)], (), (partial, late))
    picked_parts = plane_gather(picked[:96], picked[96:])
    offdiag, offdiag_low = call(
        offdiag_kernel,
        offdiag_slots,
        (*picked_parts[0], *picked_parts[1], right),
        [((768, BLK), jnp.float32), ((256, 384), bf16)],
        [
            pltpu.VMEM((N_COL, 96, 384), bf16),
            pltpu.VMEM((N_COL, 96, 384), bf16),
            pltpu.VMEM((N_ROW, 768, BLK), bf16),
            pltpu.VMEM((256, 384), jnp.float32),
            pltpu.SemaphoreType.DMA((11,)),
        ],
    )
    offdiag_low = lax.optimization_barrier((offdiag_low, late))[0]
    line = ring_parts(offdiag_low, along_z, True)
    ready = lax.optimization_barrier((line, root_inverse))[0]
    parts = line + [permute(part, other_core) for part in ready]
    (child_inverse,) = call(
        child_kernel,
        (slots, part_slots),
        (*parts, child_left, right),
        [((1024, BLK), jnp.float32)],
        [
            pltpu.VMEM((N_COL, 1536, BLK), bf16),
            pltpu.VMEM((N_ROW, 768, BLK), bf16),
            pltpu.VMEM((N_ROW, 256, 384), bf16),
            pltpu.VMEM((2, 256, 256), jnp.float32),
            pltpu.SemaphoreType.DMA((13,)),
        ],
    )
    return (
        root_inverse.reshape(6, 1, BLK, 3, 1, BLK),
        offdiag.reshape(child_block.shape),
        child_inverse.reshape(child_factor.shape),
    )


def solution(mesh):
    return jax.shard_map(
        per_device,
        mesh=mesh,
        in_specs=(
            P(None, ("half", "row"), None, None, "col", None),
            P(None, ("half", "row"), None),
            P("half", None, "row", None, None, "col", None),
            P("half", None, "row", None),
            P("half", None, "row", None, None, "col", None),
            P("half", None),
        ),
        out_specs=(
            P(None, "row", None, None, "col", None),
            P("half", None, "row", None, None, "col", None),
            P("half", None, "row", None, None, "col", None),
        ),
        check_vma=False,
    )
```

```python
import functools

import jax
import jax.numpy as jnp
from jax import lax
from jax.experimental import pallas as pl
from jax.experimental.pallas import tpu as pltpu
from jax.sharding import PartitionSpec as P

AXES = ("half", "row", "col")
N_HALF, N_ROW, N_COL = 2, 8, 16
SIDE = 4
BLK = 128
REACH = 64
ROOT_PAIRS = [(0, 0), (1, 0), (1, 1), (2, 0), (2, 1), (2, 2)]
CHILD_PAIRS = [(0, 0), (1, 0), (2, 0), (2, 1), (3, 0), (3, 1)]
VMEM_LIMIT = 60 * 1024 * 1024


def permute(array, target):
    pairs = []
    for half in range(N_HALF):
        for row in range(N_ROW):
            for col in range(N_COL):
                to_half, to_row, to_col = target(half, row, col)
                pairs.append(
                    (
                        (half * N_ROW + row) * N_COL + col,
                        (to_half * N_ROW + to_row) * N_COL + to_col,
                    )
                )
    return lax.ppermute(array, AXES, pairs)


def along_x(step):
    return lambda h, r, q: (h, r, q // SIDE * SIDE + (q + step) % SIDE)


def along_y(step):
    return lambda h, r, q: (h, r, (q + SIDE * step) % N_COL)


def along_z(step):
    return lambda h, r, q: (h, (r + 2 * step) % N_ROW, q)


def other_core(h, r, q):
    return (h, r ^ 1, q)


def other_half(h, r, q):
    return (1 - h, r, q)


def mixed(r, p):
    return (r // 2 - p // 2) % SIDE * 2 + (r ^ p) % 2


def transposed_place(h, r, q):
    return (h, q % N_ROW, q // N_ROW * N_ROW + mixed(r, q % N_ROW))


def ring_parts(own, along, split):
    before = permute(own, along(1))
    after = permute(own, along(-1))
    if not split:
        return [own, after, permute(before, along(1)), before]
    cut = own.shape[0] // 2
    return [own, after, permute(before[:cut], along(1)), permute(after[cut:], along(-1)), before]


def plane_gather(first, second):
    one = jnp.stack(ring_parts(first, along_x, False))
    two = jnp.stack(ring_parts(second, along_y, False))
    return ring_parts(one, along_y, True), ring_parts(two, along_x, True)


def dot(left, right):
    return jnp.dot(left, right, preferred_element_type=jnp.float32)


def dot_nt(left, right):
    return lax.dot_general(left, right, (((1,), (1,)), ((), ())), preferred_element_type=jnp.float32)


def cat(parts, axis):
    return jnp.concatenate(parts, axis)


def load(pairs, sems):
    copies = [pltpu.make_async_copy(src, dst, sems.at[i]) for i, (src, dst) in enumerate(pairs)]
    for copy in copies:
        copy.start()
    for copy in copies:
        copy.wait()


def spread(parts, held):
    at = 0
    pairs = []
    for part in parts:
        pairs.append((part, held.at[pl.ds(at, part.shape[0])]))
        at += part.shape[0]
    return pairs


def chooser(ref, i):
    lanes = lax.broadcasted_iota(jnp.int32, (REACH, BLK), 1)
    return jnp.where(ref[pl.ds(i * REACH, REACH), :] == lanes, 1.0, 0.0).astype(jnp.bfloat16)


def pick(low_ref, ref, picked_ref):
    rows = cat(
        [dot(chooser(ref, i), low_ref[pl.ds(i * BLK, BLK), :]).astype(jnp.bfloat16) for i in range(6)], 0
    )
    for i in range(3):
        picked_ref[pl.ds(i * REACH, REACH), :] = dot_nt(
            chooser(ref, 6 + i), rows[:, i * BLK : (i + 1) * BLK]
        ).astype(jnp.bfloat16)


def prepare_kernel(shared, *refs):
    root_ref, root_scale, child_ref, child_scale, block_ref = refs[:5]
    turned_refs, right_refs = (refs[5:7], refs[7:]) if shared == 1 else (refs[5:6] * 2, refs[6:])
    if len(right_refs) == 1:
        right_refs = right_refs * 2
    turned_base = 0 if shared == 1 else 768
    right_base = 768 if shared == 1 else 0

    def tile(ref, i, j):
        return ref[pl.ds(i * BLK, BLK), pl.ds(j * BLK, BLK)]

    def factor(ref, scale_ref, pairs, turned, right, turned_at, right_at):
        for i, (a, b) in enumerate(pairs):
            scale = jnp.broadcast_to(scale_ref[pl.ds(a, 1), :], (BLK, BLK)).T
            own = tile(ref, a, b)
            turned[pl.ds(turned_at + i * BLK, BLK), :] = own.T
            right[pl.ds(right_at + i * BLK, BLK), :] = (scale * own.astype(jnp.float32)).astype(
                jnp.bfloat16
            )

    factor(root_ref, root_scale, ROOT_PAIRS, turned_refs[0], right_refs[0], 0, 0)
    factor(child_ref, child_scale, CHILD_PAIRS, turned_refs[1], right_refs[1], turned_base, right_base)
    sort = [block_ref[pl.ds(REACH * a, REACH), :] for a in (0, 2, 4, 1, 3, 5)]
    for j in range(3):
        pair = cat(sort[2 * j : 2 * j + 2], 0)
        for i in range(2):
            at = 768 + j * 2 * BLK + i * BLK
            turned_refs[1][pl.ds(turned_base + at, BLK), :] = tile(block_ref, j, i).T
            right_refs[1][pl.ds(right_base + at, BLK), :] = pair[:, i * BLK : (i + 1) * BLK].T


def root_kernel(slot_one, slot_two, *refs):
    parts, right_in, other_picks, my_picks = refs[:10], refs[10], refs[11], refs[12]
    out_ref, theirs_ref, mine_ref, one_ref, two_ref, right_ref, acc, sems = refs[13:]
    right_in = right_in.at[:, pl.ds(0, 768), :]
    load(spread(parts[:5], one_ref) + spread(parts[5:], two_ref) + [(right_in, right_ref)], sems)
    acc[...] = jnp.zeros_like(acc)

    def step(i):
        pair = (2 * i, 2 * i + 1)
        right = [[right_ref[r, pl.ds(BLK * k, BLK), :] for k in range(6)] for r in pair]
        right_0 = cat([right[0][0], right[1][0]], 0)
        right_1 = cat([cat(right[k][1:3], 1) for k in range(2)], 0)
        right_2 = cat([cat(right[k][3:6], 1) for k in range(2)], 0)
        for side in range(2):
            one = [slot_one[side * N_ROW + r] for r in pair]
            two = [slot_two[side * N_ROW + r] for r in pair]
            left_1 = cat([one_ref[one[k]] for k in range(2)], 1)
            left_2 = cat([two_ref[two[k]] for k in range(2)], 1)
            acc[side] += dot(left_2, right_2)
            acc[side, : 2 * BLK, : 2 * BLK] += dot(left_1[BLK:], right_1)
            acc[side, :BLK, :BLK] += dot(left_1[:BLK], right_0)

    for i in range(N_ROW // 2):
        step(i)
    for outer in range(3):
        for side in range(2):
            out_ref[pl.ds((2 * outer + side) * BLK, BLK), :] = acc[
                side, pl.ds(outer * BLK, BLK), :
            ].astype(out_ref.dtype)
    pick(out_ref, other_picks, theirs_ref)
    pick(out_ref, my_picks, mine_ref)


def sum_kernel(mine_ref, other_ref, out_ref):
    for i in range(3):
        lanes = pl.ds(i * BLK, BLK)
        out_ref[pl.ds(i, 768, stride=3), :] = mine_ref[:, lanes].astype(jnp.float32) + other_ref[
            :, lanes
        ].astype(jnp.float32)


def offdiag_kernel(slot_one, slot_two, *refs):
    parts, (right_in, out_ref, low_ref, one_ref, two_ref, block_ref, acc, sems) = refs[:10], refs[10:]
    block_in = right_in.at[:, pl.ds(1536, 768), :]
    load(spread(parts[:5], one_ref) + spread(parts[5:], two_ref) + [(block_in, block_ref)], sems)
    acc[...] = jnp.zeros_like(acc)

    def step(r):
        left = cat([block_ref[r, pl.ds(256 * i, 256), :] for i in range(3)], 1)
        right = cat(
            [
                one_ref[slot_one[r]],
                two_ref[slot_two[r]],
                one_ref[slot_one[N_ROW + r]],
                two_ref[slot_two[N_ROW + r]],
            ],
            0,
        )
        acc[...] += dot(left, right)

    for i in range(N_ROW):
        step(i)
    total = -acc[...]
    low_ref[...] = total.astype(low_ref.dtype)
    for i in range(2):
        out_ref[pl.ds(i, 384, stride=2), :] = total[i * BLK : (i + 1) * BLK, :].T


def child_kernel(slots, part_slots, *refs):
    parts, (left_in, right_in, out_ref, left_ref, factor_ref, right_ref, acc, sems) = refs[:10], refs[10:]
    first, second = pl.ds(0, 768), pl.ds(768, 768)
    pairs = [
        (left_in.at[:, first, :], left_ref.at[:, first, :]),
        (right_in.at[:, pl.ds(768, 768), :], factor_ref),
        (left_in.at[:, second, :], left_ref.at[:, second, :]),
    ]
    at = 0
    for part in parts:
        pairs.append((part, right_ref.at[at // 256, pl.ds(at % 256, part.shape[0]), :]))
        at += part.shape[0]
    copies = [pltpu.make_async_copy(src, dst, sems.at[i]) for i, (src, dst) in enumerate(pairs)]
    for copy in copies:
        copy.start()
    acc[...] = jnp.zeros_like(acc)
    for copy in copies[:2]:
        copy.wait()

    def own(r):
        right = [factor_ref[r, pl.ds(BLK * i, BLK), :] for i in range(6)]
        right_0 = cat(right[0:2], 0)
        right_1 = cat([cat(right[2:4], 1), cat(right[4:6], 1)], 0)
        for side in range(2):
            slot = slots[side * N_ROW + r]
            left_0 = cat([left_ref[slot, :BLK, :], left_ref[slot, BLK : 2 * BLK, :]], 1)
            left_1 = cat([left_ref[slot, 2 * BLK : 4 * BLK, :], left_ref[slot, 4 * BLK : 6 * BLK, :]], 1)
            acc[side] += dot(left_1, right_1)
            acc[side, :BLK, :BLK] += dot(left_0, right_0)

    for r in range(N_ROW):
        own(r)
    for copy in copies[2:]:
        copy.wait()

    def coupled(i):
        pair = (2 * i, 2 * i + 1)
        right = cat([right_ref[part_slots[r]] for r in pair], 1)
        for side in range(2):
            held = [slots[side * N_ROW + r] for r in pair]
            left = cat([left_ref[slot, pl.ds(768 + 256 * k, 256), :] for slot in held for k in range(3)], 1)
            acc[side] -= dot_nt(left, right)

    for i in range(N_ROW // 2):
        coupled(i)
    for outer in range(2):
        for side in range(2):
            for i in range(2):
                at = (2 * outer + side) * 2 * BLK + i
                out_ref[pl.ds(at, BLK, stride=2), :] = acc[
                    side, pl.ds(outer * BLK, BLK), pl.ds(i * BLK, BLK)
                ]


def call(kernel, scalars, arrays, outs, scratch, blocks=()):
    vmem = pl.BlockSpec(memory_space=pltpu.VMEM)
    smem = pl.BlockSpec(memory_space=pltpu.SMEM)
    anywhere = pl.BlockSpec(memory_space=pl.ANY)
    return pl.pallas_call(
        kernel,
        in_specs=[smem] * len(scalars) + [anywhere] * len(arrays) + [vmem] * len(blocks),
        out_specs=[vmem] * len(outs),
        out_shape=[jax.ShapeDtypeStruct(*o) for o in outs],
        scratch_shapes=list(scratch),
        compiler_params=pltpu.CompilerParams(vmem_limit_bytes=VMEM_LIMIT),
    )(*scalars, *arrays, *blocks)


def per_device(root_factor, root_pivots, child_factor, child_pivots, child_block, child_rows):
    row = lax.axis_index("row")
    col = lax.axis_index("col")
    bf16 = jnp.bfloat16
    root_turned, child_turned, right_here = call(
        functools.partial(prepare_kernel, 1),
        (),
        (),
        [((768, BLK), bf16), ((1536, BLK), bf16), ((2304, BLK), bf16)],
        (),
        (
            root_factor.reshape(384, 384),
            root_pivots.reshape(3, BLK),
            child_factor.reshape(512, 256),
            child_pivots.reshape(4, BLK),
            child_block.reshape(384, 256),
        ),
    )
    turned = permute(root_turned, transposed_place)
    right = lax.all_gather(right_here, "row", axis=0, tiled=False)

    rows = child_rows[0].reshape(48, REACH) % BLK
    row_picks = lax.dynamic_index_in_dim(rows.reshape(6, N_ROW, REACH), row, 1, keepdims=False)
    col_picks = lax.dynamic_index_in_dim(rows.reshape(3, N_COL, REACH), col, 1, keepdims=False)
    my_picks = jnp.concatenate([row_picks.reshape(-1), col_picks.reshape(-1)])[:, None]
    other_picks = permute(my_picks, other_half)
    child_turned = lax.optimization_barrier((child_turned, other_picks))[0]
    child_here = permute(child_turned, transposed_place)

    side = jnp.arange(2, dtype=jnp.int32)[:, None]
    classes = jnp.arange(N_ROW, dtype=jnp.int32)[None, :]
    source = side * N_ROW + mixed(classes, row)
    my_x, my_y = col % SIDE, col // SIDE

    def plane_slots(place):
        dx = (place % SIDE - my_x) % SIDE
        dy = (place // SIDE - my_y) % SIDE
        return (dy * SIDE + dx).reshape(-1), (dx * SIDE + dy).reshape(-1)

    root_slots = plane_slots(source)
    offdiag_slots = plane_slots(side * N_ROW + classes)
    slots = source.reshape(-1)
    r = classes[0]
    part_slots = ((r ^ row) & 1) * SIDE + (r // 2 - row // 2) % SIDE
    turned, root_slots, offdiag_slots, slots, part_slots, my_picks, other_picks = lax.optimization_barrier(
        (turned, root_slots, offdiag_slots, slots, part_slots, my_picks, other_picks)
    )
    root_parts = plane_gather(turned[:384], turned[384:])
    child_here = lax.optimization_barrier((child_here, root_parts))[0]
    child_left = lax.all_gather(child_here, "col", axis=0, tiled=False)

    partial, theirs, mine = call(
        root_kernel,
        root_slots,
        (*root_parts[0], *root_parts[1], right),
        [((768, 384), bf16), ((192, 384), bf16), ((192, 384), bf16)],
        [
            pltpu.VMEM((N_COL, 384, BLK), bf16),
            pltpu.VMEM((N_COL, 384, BLK), bf16),
            pltpu.VMEM((N_ROW, 768, BLK), bf16),
            pltpu.VMEM((2, 384, 384), jnp.float32),
            pltpu.SemaphoreType.DMA((11,)),
        ],
        (other_picks, my_picks),
    )
    theirs = permute(theirs, other_half)
    picked = (mine.astype(jnp.float32) + theirs.astype(jnp.float32)).astype(bf16)
    late = lax.optimization_barrier((partial, picked))[0]
    late = permute(late, other_half)
    (root_inverse,) = call(sum_kernel, (), (), [((2304, BLK), jnp.float32)], (), (partial, late))
    picked_parts = plane_gather(picked[:96], picked[96:])
    offdiag, offdiag_low = call(
        offdiag_kernel,
        offdiag_slots,
        (*picked_parts[0], *picked_parts[1], right),
        [((768, BLK), jnp.float32), ((256, 384), bf16)],
        [
            pltpu.VMEM((N_COL, 96, 384), bf16),
            pltpu.VMEM((N_COL, 96, 384), bf16),
            pltpu.VMEM((N_ROW, 768, BLK), bf16),
            pltpu.VMEM((256, 384), jnp.float32),
            pltpu.SemaphoreType.DMA((11,)),
        ],
    )
    offdiag_low = lax.optimization_barrier((offdiag_low, late))[0]
    line = ring_parts(offdiag_low, along_z, True)
    ready = lax.optimization_barrier((line, root_inverse))[0]
    parts = line + [permute(part, other_core) for part in ready]
    (child_inverse,) = call(
        child_kernel,
        (slots, part_slots),
        (*parts, child_left, right),
        [((1024, BLK), jnp.float32)],
        [
            pltpu.VMEM((N_COL, 1536, BLK), bf16),
            pltpu.VMEM((N_ROW, 768, BLK), bf16),
            pltpu.VMEM((N_ROW, 256, 384), bf16),
            pltpu.VMEM((2, 256, 256), jnp.float32),
            pltpu.SemaphoreType.DMA((13,)),
        ],
    )
    return (
        root_inverse.reshape(6, 1, BLK, 3, 1, BLK),
        offdiag.reshape(child_block.shape),
        child_inverse.reshape(child_factor.shape),
    )


def solution(mesh):
    return jax.shard_map(
        per_device,
        mesh=mesh,
        in_specs=(
            P(None, ("half", "row"), None, None, "col", None),
            P(None, ("half", "row"), None),
            P("half", None, "row", None, None, "col", None),
            P("half", None, "row", None),
            P("half", None, "row", None, None, "col", None),
            P("half", None),
        ),
        out_specs=(
            P(None, "row", None, None, "col", None),
            P("half", None, "row", None, None, "col", None),
            P("half", None, "row", None, None, "col", None),
        ),
        check_vma=False,
    )
```

```python
import functools

import jax
import jax.numpy as jnp
from jax import lax
from jax.experimental import pallas as pl
from jax.experimental.pallas import tpu as pltpu
from jax.sharding import PartitionSpec as P

AXES = ("half", "row", "col")
N_HALF, N_ROW, N_COL = 2, 8, 16
SIDE = 4
BLK = 128
REACH = 64
ROOT_PAIRS = [(0, 0), (1, 0), (1, 1), (2, 0), (2, 1), (2, 2)]
CHILD_PAIRS = [(0, 0), (1, 0), (2, 0), (2, 1), (3, 0), (3, 1)]
VMEM_LIMIT = 60 * 1024 * 1024


def permute(array, target):
    pairs = []
    for half in range(N_HALF):
        for row in range(N_ROW):
            for col in range(N_COL):
                to_half, to_row, to_col = target(half, row, col)
                pairs.append(
                    (
                        (half * N_ROW + row) * N_COL + col,
                        (to_half * N_ROW + to_row) * N_COL + to_col,
                    )
                )
    return lax.ppermute(array, AXES, pairs)


def along_x(step):
    return lambda h, r, q: (h, r, q // SIDE * SIDE + (q + step) % SIDE)


def along_y(step):
    return lambda h, r, q: (h, r, (q + SIDE * step) % N_COL)


def along_z(step):
    return lambda h, r, q: (h, (r + 2 * step) % N_ROW, q)


def other_core(h, r, q):
    return (h, r ^ 1, q)


def other_half(h, r, q):
    return (1 - h, r, q)


def mixed(r, p):
    return (r // 2 - p // 2) % SIDE * 2 + (r ^ p) % 2


def transposed_place(h, r, q):
    return (h, q % N_ROW, q // N_ROW * N_ROW + mixed(r, q % N_ROW))


def ring_parts(own, along, split):
    before = permute(own, along(1))
    after = permute(own, along(-1))
    if not split:
        return [own, after, permute(before, along(1)), before]
    cut = own.shape[0] // 2
    return [own, after, permute(before[:cut], along(1)), permute(after[cut:], along(-1)), before]


def plane_gather(first, second):
    one = jnp.stack(ring_parts(first, along_x, False))
    two = jnp.stack(ring_parts(second, along_y, False))
    return ring_parts(one, along_y, True), ring_parts(two, along_x, True)


def dot(left, right):
    return jnp.dot(left, right, preferred_element_type=jnp.float32)


def dot_nt(left, right):
    return lax.dot_general(left, right, (((1,), (1,)), ((), ())), preferred_element_type=jnp.float32)


def cat(parts, axis):
    return jnp.concatenate(parts, axis)


def load(pairs, sems):
    copies = [pltpu.make_async_copy(src, dst, sems.at[i]) for i, (src, dst) in enumerate(pairs)]
    for copy in copies:
        copy.start()
    for copy in copies:
        copy.wait()


def spread(parts, held):
    at = 0
    pairs = []
    for part in parts:
        pairs.append((part, held.at[pl.ds(at, part.shape[0])]))
        at += part.shape[0]
    return pairs


def chooser(ref, i):
    lanes = lax.broadcasted_iota(jnp.int32, (REACH, BLK), 1)
    return jnp.where(ref[pl.ds(i * REACH, REACH), :] == lanes, 1.0, 0.0).astype(jnp.bfloat16)


def pick(low_ref, ref, picked_ref):
    rows = cat(
        [dot(chooser(ref, i), low_ref[pl.ds(i * BLK, BLK), :]).astype(jnp.bfloat16) for i in range(6)], 0
    )
    for i in range(3):
        picked_ref[pl.ds(i * REACH, REACH), :] = dot_nt(
            chooser(ref, 6 + i), rows[:, i * BLK : (i + 1) * BLK]
        ).astype(jnp.bfloat16)


def prepare_kernel(shared, *refs):
    root_ref, root_scale, child_ref, child_scale, block_ref = refs[:5]
    turned_refs, right_refs = (refs[5:7], refs[7:]) if shared == 1 else (refs[5:6] * 2, refs[6:])
    if len(right_refs) == 1:
        right_refs = right_refs * 2
    turned_base = 0 if shared == 1 else 768
    right_base = 768 if shared == 1 else 0

    def tile(ref, i, j):
        return ref[pl.ds(i * BLK, BLK), pl.ds(j * BLK, BLK)]

    def factor(ref, scale_ref, pairs, turned, right, turned_at, right_at):
        for i, (a, b) in enumerate(pairs):
            scale = jnp.broadcast_to(scale_ref[pl.ds(a, 1), :], (BLK, BLK)).T
            own = tile(ref, a, b)
            turned[pl.ds(turned_at + i * BLK, BLK), :] = own.T
            right[pl.ds(right_at + i * BLK, BLK), :] = (scale * own.astype(jnp.float32)).astype(
                jnp.bfloat16
            )

    factor(root_ref, root_scale, ROOT_PAIRS, turned_refs[0], right_refs[0], 0, 0)
    factor(child_ref, child_scale, CHILD_PAIRS, turned_refs[1], right_refs[1], turned_base, right_base)
    sort = [block_ref[pl.ds(REACH * a, REACH), :] for a in (0, 2, 4, 1, 3, 5)]
    for j in range(3):
        pair = cat(sort[2 * j : 2 * j + 2], 0)
        for i in range(2):
            at = 768 + j * 2 * BLK + i * BLK
            turned_refs[1][pl.ds(turned_base + at, BLK), :] = tile(block_ref, j, i).T
            right_refs[1][pl.ds(right_base + at, BLK), :] = pair[:, i * BLK : (i + 1) * BLK].T


def root_kernel(slot_one, slot_two, *refs):
    parts, right_in, other_picks, my_picks = refs[:10], refs[10], refs[11], refs[12]
    out_ref, theirs_ref, mine_ref, one_ref, two_ref, right_ref, acc, sems = refs[13:]
    right_in = right_in.at[:, pl.ds(0, 768), :]
    load(spread(parts[:5], one_ref) + spread(parts[5:], two_ref) + [(right_in, right_ref)], sems)
    acc[...] = jnp.zeros_like(acc)

    def step(i):
        pair = (2 * i, 2 * i + 1)
        right = [[right_ref[r, pl.ds(BLK * k, BLK), :] for k in range(6)] for r in pair]
        right_0 = cat([right[0][0], right[1][0]], 0)
        right_1 = cat([cat(right[k][1:3], 1) for k in range(2)], 0)
        right_2 = cat([cat(right[k][3:6], 1) for k in range(2)], 0)
        for side in range(2):
            one = [slot_one[side * N_ROW + r] for r in pair]
            two = [slot_two[side * N_ROW + r] for r in pair]
            left_1 = cat([one_ref[one[k]] for k in range(2)], 1)
            left_2 = cat([two_ref[two[k]] for k in range(2)], 1)
            acc[side] += dot(left_2, right_2)
            acc[side, : 2 * BLK, : 2 * BLK] += dot(left_1[BLK:], right_1)
            acc[side, :BLK, :BLK] += dot(left_1[:BLK], right_0)

    for i in range(N_ROW // 2):
        step(i)
    for outer in range(3):
        for side in range(2):
            out_ref[pl.ds((2 * outer + side) * BLK, BLK), :] = acc[
                side, pl.ds(outer * BLK, BLK), :
            ].astype(out_ref.dtype)
    pick(out_ref, other_picks, theirs_ref)
    pick(out_ref, my_picks, mine_ref)


def sum_kernel(mine_ref, other_ref, out_ref):
    for i in range(3):
        lanes = pl.ds(i * BLK, BLK)
        out_ref[pl.ds(i, 768, stride=3), :] = mine_ref[:, lanes].astype(jnp.float32) + other_ref[
            :, lanes
        ].astype(jnp.float32)


def offdiag_kernel(slot_one, slot_two, *refs):
    parts, (right_in, out_ref, low_ref, one_ref, two_ref, block_ref, acc, sems) = refs[:10], refs[10:]
    block_in = right_in.at[:, pl.ds(1536, 768), :]
    load(spread(parts[:5], one_ref) + spread(parts[5:], two_ref) + [(block_in, block_ref)], sems)
    acc[...] = jnp.zeros_like(acc)

    def step(r):
        left = cat([block_ref[r, pl.ds(256 * i, 256), :] for i in range(3)], 1)
        right = cat(
            [
                one_ref[slot_one[r]],
                two_ref[slot_two[r]],
                one_ref[slot_one[N_ROW + r]],
                two_ref[slot_two[N_ROW + r]],
            ],
            0,
        )
        acc[...] += dot(left, right)

    for i in range(N_ROW):
        step(i)
    total = -acc[...]
    low_ref[...] = total.astype(low_ref.dtype)
    for i in range(2):
        out_ref[pl.ds(i, 384, stride=2), :] = total[i * BLK : (i + 1) * BLK, :].T


def child_kernel(slots, part_slots, *refs):
    parts, (left_in, right_in, out_ref, left_ref, factor_ref, right_ref, acc, sems) = refs[:10], refs[10:]
    first, second = pl.ds(0, 768), pl.ds(768, 768)
    pairs = [
        (left_in.at[:, first, :], left_ref.at[:, first, :]),
        (right_in.at[:, pl.ds(768, 768), :], factor_ref),
        (left_in.at[:, second, :], left_ref.at[:, second, :]),
    ]
    at = 0
    for part in parts:
        pairs.append((part, right_ref.at[at // 256, pl.ds(at % 256, part.shape[0]), :]))
        at += part.shape[0]
    copies = [pltpu.make_async_copy(src, dst, sems.at[i]) for i, (src, dst) in enumerate(pairs)]
    for copy in copies:
        copy.start()
    acc[...] = jnp.zeros_like(acc)
    for copy in copies[:2]:
        copy.wait()

    def own(r):
        right = [factor_ref[r, pl.ds(BLK * i, BLK), :] for i in range(6)]
        right_0 = cat(right[0:2], 0)
        right_1 = cat([cat(right[2:4], 1), cat(right[4:6], 1)], 0)
        for side in range(2):
            slot = slots[side * N_ROW + r]
            left_0 = cat([left_ref[slot, :BLK, :], left_ref[slot, BLK : 2 * BLK, :]], 1)
            left_1 = cat([left_ref[slot, 2 * BLK : 4 * BLK, :], left_ref[slot, 4 * BLK : 6 * BLK, :]], 1)
            acc[side] += dot(left_1, right_1)
            acc[side, :BLK, :BLK] += dot(left_0, right_0)

    for r in range(N_ROW):
        own(r)
    for copy in copies[2:]:
        copy.wait()

    def coupled(i):
        pair = (2 * i, 2 * i + 1)
        right = cat([right_ref[part_slots[r]] for r in pair], 1)
        for side in range(2):
            held = [slots[side * N_ROW + r] for r in pair]
            left = cat([left_ref[slot, pl.ds(768 + 256 * k, 256), :] for slot in held for k in range(3)], 1)
            acc[side] -= dot_nt(left, right)

    for i in range(N_ROW // 2):
        coupled(i)
    for outer in range(2):
        for side in range(2):
            for i in range(2):
                at = (2 * outer + side) * 2 * BLK + i
                out_ref[pl.ds(at, BLK, stride=2), :] = acc[
                    side, pl.ds(outer * BLK, BLK), pl.ds(i * BLK, BLK)
                ]


def call(kernel, scalars, arrays, outs, scratch, blocks=()):
    vmem = pl.BlockSpec(memory_space=pltpu.VMEM)
    smem = pl.BlockSpec(memory_space=pltpu.SMEM)
    anywhere = pl.BlockSpec(memory_space=pl.ANY)
    return pl.pallas_call(
        kernel,
        in_specs=[smem] * len(scalars) + [anywhere] * len(arrays) + [vmem] * len(blocks),
        out_specs=[vmem] * len(outs),
        out_shape=[jax.ShapeDtypeStruct(*o) for o in outs],
        scratch_shapes=list(scratch),
        compiler_params=pltpu.CompilerParams(vmem_limit_bytes=VMEM_LIMIT),
    )(*scalars, *arrays, *blocks)


def per_device(root_factor, root_pivots, child_factor, child_pivots, child_block, child_rows):
    row = lax.axis_index("row")
    col = lax.axis_index("col")
    bf16 = jnp.bfloat16
    root_turned, child_turned, right_here = call(
        functools.partial(prepare_kernel, 1),
        (),
        (),
        [((768, BLK), bf16), ((1536, BLK), bf16), ((2304, BLK), bf16)],
        (),
        (
            root_factor.reshape(384, 384),
            root_pivots.reshape(3, BLK),
            child_factor.reshape(512, 256),
            child_pivots.reshape(4, BLK),
            child_block.reshape(384, 256),
        ),
    )
    turned = permute(root_turned, transposed_place)
    right = lax.all_gather(right_here, "row", axis=0, tiled=False)

    rows = child_rows[0].reshape(48, REACH) % BLK
    row_picks = lax.dynamic_index_in_dim(rows.reshape(6, N_ROW, REACH), row, 1, keepdims=False)
    col_picks = lax.dynamic_index_in_dim(rows.reshape(3, N_COL, REACH), col, 1, keepdims=False)
    my_picks = jnp.concatenate([row_picks.reshape(-1), col_picks.reshape(-1)])[:, None]
    other_picks = permute(my_picks, other_half)
    child_turned = lax.optimization_barrier((child_turned, other_picks))[0]
    child_here = permute(child_turned, transposed_place)

    side = jnp.arange(2, dtype=jnp.int32)[:, None]
    classes = jnp.arange(N_ROW, dtype=jnp.int32)[None, :]
    source = side * N_ROW + mixed(classes, row)
    my_x, my_y = col % SIDE, col // SIDE

    def plane_slots(place):
        dx = (place % SIDE - my_x) % SIDE
        dy = (place // SIDE - my_y) % SIDE
        return (dy * SIDE + dx).reshape(-1), (dx * SIDE + dy).reshape(-1)

    root_slots = plane_slots(source)
    offdiag_slots = plane_slots(side * N_ROW + classes)
    slots = source.reshape(-1)
    r = classes[0]
    part_slots = ((r ^ row) & 1) * SIDE + (r // 2 - row // 2) % SIDE
    turned, root_slots, offdiag_slots, slots, part_slots, my_picks, other_picks = lax.optimization_barrier(
        (turned, root_slots, offdiag_slots, slots, part_slots, my_picks, other_picks)
    )
    root_parts = plane_gather(turned[:384], turned[384:])

    partial, theirs, mine = call(
        root_kernel,
        root_slots,
        (*root_parts[0], *root_parts[1], right),
        [((768, 384), bf16), ((192, 384), bf16), ((192, 384), bf16)],
        [
            pltpu.VMEM((N_COL, 384, BLK), bf16),
            pltpu.VMEM((N_COL, 384, BLK), bf16),
            pltpu.VMEM((N_ROW, 768, BLK), bf16),
            pltpu.VMEM((2, 384, 384), jnp.float32),
            pltpu.SemaphoreType.DMA((11,)),
        ],
        (other_picks, my_picks),
    )
    child_here = lax.optimization_barrier((child_here, partial))[0]
    child_left = lax.all_gather(child_here, "col", axis=0, tiled=False)
    theirs = permute(theirs, other_half)
    picked = (mine.astype(jnp.float32) + theirs.astype(jnp.float32)).astype(bf16)
    late = lax.optimization_barrier((partial, picked))[0]
    late = permute(late, other_half)
    (root_inverse,) = call(sum_kernel, (), (), [((2304, BLK), jnp.float32)], (), (partial, late))
    picked_parts = plane_gather(picked[:96], picked[96:])
    offdiag, offdiag_low = call(
        offdiag_kernel,
        offdiag_slots,
        (*picked_parts[0], *picked_parts[1], right),
        [((768, BLK), jnp.float32), ((256, 384), bf16)],
        [
            pltpu.VMEM((N_COL, 96, 384), bf16),
            pltpu.VMEM((N_COL, 96, 384), bf16),
            pltpu.VMEM((N_ROW, 768, BLK), bf16),
            pltpu.VMEM((256, 384), jnp.float32),
            pltpu.SemaphoreType.DMA((11,)),
        ],
    )
    offdiag_low = lax.optimization_barrier((offdiag_low, late))[0]
    line = ring_parts(offdiag_low, along_z, True)
    ready = lax.optimization_barrier((line, root_inverse))[0]
    parts = line + [permute(part, other_core) for part in ready]
    (child_inverse,) = call(
        child_kernel,
        (slots, part_slots),
        (*parts, child_left, right),
        [((1024, BLK), jnp.float32)],
        [
            pltpu.VMEM((N_COL, 1536, BLK), bf16),
            pltpu.VMEM((N_ROW, 768, BLK), bf16),
            pltpu.VMEM((N_ROW, 256, 384), bf16),
            pltpu.VMEM((2, 256, 256), jnp.float32),
            pltpu.SemaphoreType.DMA((13,)),
        ],
    )
    return (
        root_inverse.reshape(6, 1, BLK, 3, 1, BLK),
        offdiag.reshape(child_block.shape),
        child_inverse.reshape(child_factor.shape),
    )


def solution(mesh):
    return jax.shard_map(
        per_device,
        mesh=mesh,
        in_specs=(
            P(None, ("half", "row"), None, None, "col", None),
            P(None, ("half", "row"), None),
            P("half", None, "row", None, None, "col", None),
            P("half", None, "row", None),
            P("half", None, "row", None, None, "col", None),
            P("half", None),
        ),
        out_specs=(
            P(None, "row", None, None, "col", None),
            P("half", None, "row", None, None, "col", None),
            P("half", None, "row", None, None, "col", None),
        ),
        check_vma=False,
    )
```

```python
import functools

import jax
import jax.numpy as jnp
from jax import lax
from jax.experimental import pallas as pl
from jax.experimental.pallas import tpu as pltpu
from jax.sharding import PartitionSpec as P

AXES = ("half", "row", "col")
N_HALF, N_ROW, N_COL = 2, 8, 16
SIDE = 4
BLK = 128
REACH = 64
ROOT_PAIRS = [(0, 0), (1, 0), (1, 1), (2, 0), (2, 1), (2, 2)]
CHILD_PAIRS = [(0, 0), (1, 0), (2, 0), (2, 1), (3, 0), (3, 1)]
VMEM_LIMIT = 60 * 1024 * 1024


def permute(array, target):
    pairs = []
    for half in range(N_HALF):
        for row in range(N_ROW):
            for col in range(N_COL):
                to_half, to_row, to_col = target(half, row, col)
                pairs.append(
                    (
                        (half * N_ROW + row) * N_COL + col,
                        (to_half * N_ROW + to_row) * N_COL + to_col,
                    )
                )
    return lax.ppermute(array, AXES, pairs)


def along_x(step):
    return lambda h, r, q: (h, r, q // SIDE * SIDE + (q + step) % SIDE)


def along_y(step):
    return lambda h, r, q: (h, r, (q + SIDE * step) % N_COL)


def along_z(step):
    return lambda h, r, q: (h, (r + 2 * step) % N_ROW, q)


def other_core(h, r, q):
    return (h, r ^ 1, q)


def other_half(h, r, q):
    return (1 - h, r, q)


def mixed(r, p):
    return (r // 2 - p // 2 + r % 2 * 2) % SIDE * 2 + (r ^ p) % 2


def transposed_place(h, r, q):
    return (h, q % N_ROW, q // N_ROW * N_ROW + mixed(r, q % N_ROW))


def ring_parts(own, along, split):
    before = permute(own, along(1))
    after = permute(own, along(-1))
    if not split:
        return [own, after, permute(before, along(1)), before]
    cut = own.shape[0] // 2
    return [own, after, permute(before[:cut], along(1)), permute(after[cut:], along(-1)), before]


def plane_gather(first, second):
    one = jnp.stack(ring_parts(first, along_x, False))
    two = jnp.stack(ring_parts(second, along_y, False))
    return ring_parts(one, along_y, True), ring_parts(two, along_x, True)


def dot(left, right):
    return jnp.dot(left, right, preferred_element_type=jnp.float32)


def dot_nt(left, right):
    return lax.dot_general(left, right, (((1,), (1,)), ((), ())), preferred_element_type=jnp.float32)


def cat(parts, axis):
    return jnp.concatenate(parts, axis)


def load(pairs, sems):
    copies = [pltpu.make_async_copy(src, dst, sems.at[i]) for i, (src, dst) in enumerate(pairs)]
    for copy in copies:
        copy.start()
    for copy in copies:
        copy.wait()


def spread(parts, held):
    at = 0
    pairs = []
    for part in parts:
        pairs.append((part, held.at[pl.ds(at, part.shape[0])]))
        at += part.shape[0]
    return pairs


def chooser(ref, i):
    lanes = lax.broadcasted_iota(jnp.int32, (REACH, BLK), 1)
    return jnp.where(ref[pl.ds(i * REACH, REACH), :] == lanes, 1.0, 0.0).astype(jnp.bfloat16)


def pick(low_ref, ref, picked_ref):
    rows = cat(
        [dot(chooser(ref, i), low_ref[pl.ds(i * BLK, BLK), :]).astype(jnp.bfloat16) for i in range(6)], 0
    )
    for i in range(3):
        picked_ref[pl.ds(i * REACH, REACH), :] = dot_nt(
            chooser(ref, 6 + i), rows[:, i * BLK : (i + 1) * BLK]
        ).astype(jnp.bfloat16)


def prepare_kernel(shared, *refs):
    root_ref, root_scale, child_ref, child_scale, block_ref = refs[:5]
    turned_refs, right_refs = (refs[5:7], refs[7:]) if shared == 1 else (refs[5:6] * 2, refs[6:])
    if len(right_refs) == 1:
        right_refs = right_refs * 2
    turned_base = 0 if shared == 1 else 768
    right_base = 768 if shared == 1 else 0

    def tile(ref, i, j):
        return ref[pl.ds(i * BLK, BLK), pl.ds(j * BLK, BLK)]

    def factor(ref, scale_ref, pairs, turned, right, turned_at, right_at):
        for i, (a, b) in enumerate(pairs):
            scale = jnp.broadcast_to(scale_ref[pl.ds(a, 1), :], (BLK, BLK)).T
            own = tile(ref, a, b)
            turned[pl.ds(turned_at + i * BLK, BLK), :] = own.T
            right[pl.ds(right_at + i * BLK, BLK), :] = (scale * own.astype(jnp.float32)).astype(
                jnp.bfloat16
            )

    factor(root_ref, root_scale, ROOT_PAIRS, turned_refs[0], right_refs[0], 0, 0)
    factor(child_ref, child_scale, CHILD_PAIRS, turned_refs[1], right_refs[1], turned_base, right_base)
    sort = [block_ref[pl.ds(REACH * a, REACH), :] for a in (0, 2, 4, 1, 3, 5)]
    for j in range(3):
        pair = cat(sort[2 * j : 2 * j + 2], 0)
        for i in range(2):
            at = 768 + j * 2 * BLK + i * BLK
            turned_refs[1][pl.ds(turned_base + at, BLK), :] = tile(block_ref, j, i).T
            right_refs[1][pl.ds(right_base + at, BLK), :] = pair[:, i * BLK : (i + 1) * BLK].T


def root_kernel(slot_one, slot_two, *refs):
    parts, right_in, other_picks, my_picks = refs[:10], refs[10], refs[11], refs[12]
    out_ref, theirs_ref, mine_ref, one_ref, two_ref, right_ref, acc, sems = refs[13:]
    right_in = right_in.at[:, pl.ds(0, 768), :]
    load(spread(parts[:5], one_ref) + spread(parts[5:], two_ref) + [(right_in, right_ref)], sems)
    acc[...] = jnp.zeros_like(acc)

    def step(i):
        pair = (2 * i, 2 * i + 1)
        right = [[right_ref[r, pl.ds(BLK * k, BLK), :] for k in range(6)] for r in pair]
        right_0 = cat([right[0][0], right[1][0]], 0)
        right_1 = cat([cat(right[k][1:3], 1) for k in range(2)], 0)
        right_2 = cat([cat(right[k][3:6], 1) for k in range(2)], 0)
        for side in range(2):
            one = [slot_one[side * N_ROW + r] for r in pair]
            two = [slot_two[side * N_ROW + r] for r in pair]
            left_1 = cat([one_ref[one[k]] for k in range(2)], 1)
            left_2 = cat([two_ref[two[k]] for k in range(2)], 1)
            acc[side] += dot(left_2, right_2)
            acc[side, : 2 * BLK, : 2 * BLK] += dot(left_1[BLK:], right_1)
            acc[side, :BLK, :BLK] += dot(left_1[:BLK], right_0)

    for i in range(N_ROW // 2):
        step(i)
    for outer in range(3):
        for side in range(2):
            out_ref[pl.ds((2 * outer + side) * BLK, BLK), :] = acc[
                side, pl.ds(outer * BLK, BLK), :
            ].astype(out_ref.dtype)
    pick(out_ref, other_picks, theirs_ref)
    pick(out_ref, my_picks, mine_ref)


def sum_kernel(mine_ref, other_ref, out_ref):
    for i in range(3):
        lanes = pl.ds(i * BLK, BLK)
        out_ref[pl.ds(i, 768, stride=3), :] = mine_ref[:, lanes].astype(jnp.float32) + other_ref[
            :, lanes
        ].astype(jnp.float32)


def offdiag_kernel(slot_one, slot_two, *refs):
    parts, (right_in, out_ref, low_ref, one_ref, two_ref, block_ref, acc, sems) = refs[:10], refs[10:]
    block_in = right_in.at[:, pl.ds(1536, 768), :]
    load(spread(parts[:5], one_ref) + spread(parts[5:], two_ref) + [(block_in, block_ref)], sems)
    acc[...] = jnp.zeros_like(acc)

    def step(r):
        left = cat([block_ref[r, pl.ds(256 * i, 256), :] for i in range(3)], 1)
        right = cat(
            [
                one_ref[slot_one[r]],
                two_ref[slot_two[r]],
                one_ref[slot_one[N_ROW + r]],
                two_ref[slot_two[N_ROW + r]],
            ],
            0,
        )
        acc[...] += dot(left, right)

    for i in range(N_ROW):
        step(i)
    total = -acc[...]
    low_ref[...] = total.astype(low_ref.dtype)
    for i in range(2):
        out_ref[pl.ds(i, 384, stride=2), :] = total[i * BLK : (i + 1) * BLK, :].T


def child_kernel(slots, part_slots, *refs):
    parts, (left_in, right_in, out_ref, left_ref, factor_ref, right_ref, acc, sems) = refs[:10], refs[10:]
    first, second = pl.ds(0, 768), pl.ds(768, 768)
    pairs = [
        (left_in.at[:, first, :], left_ref.at[:, first, :]),
        (right_in.at[:, pl.ds(768, 768), :], factor_ref),
        (left_in.at[:, second, :], left_ref.at[:, second, :]),
    ]
    at = 0
    for part in parts:
        pairs.append((part, right_ref.at[at // 256, pl.ds(at % 256, part.shape[0]), :]))
        at += part.shape[0]
    copies = [pltpu.make_async_copy(src, dst, sems.at[i]) for i, (src, dst) in enumerate(pairs)]
    for copy in copies:
        copy.start()
    acc[...] = jnp.zeros_like(acc)
    for copy in copies[:2]:
        copy.wait()

    def own(r):
        right = [factor_ref[r, pl.ds(BLK * i, BLK), :] for i in range(6)]
        right_0 = cat(right[0:2], 0)
        right_1 = cat([cat(right[2:4], 1), cat(right[4:6], 1)], 0)
        for side in range(2):
            slot = slots[side * N_ROW + r]
            left_0 = cat([left_ref[slot, :BLK, :], left_ref[slot, BLK : 2 * BLK, :]], 1)
            left_1 = cat([left_ref[slot, 2 * BLK : 4 * BLK, :], left_ref[slot, 4 * BLK : 6 * BLK, :]], 1)
            acc[side] += dot(left_1, right_1)
            acc[side, :BLK, :BLK] += dot(left_0, right_0)

    for r in range(N_ROW):
        own(r)
    for copy in copies[2:]:
        copy.wait()

    def coupled(i):
        pair = (2 * i, 2 * i + 1)
        right = cat([right_ref[part_slots[r]] for r in pair], 1)
        for side in range(2):
            held = [slots[side * N_ROW + r] for r in pair]
            left = cat([left_ref[slot, pl.ds(768 + 256 * k, 256), :] for slot in held for k in range(3)], 1)
            acc[side] -= dot_nt(left, right)

    for i in range(N_ROW // 2):
        coupled(i)
    for outer in range(2):
        for side in range(2):
            for i in range(2):
                at = (2 * outer + side) * 2 * BLK + i
                out_ref[pl.ds(at, BLK, stride=2), :] = acc[
                    side, pl.ds(outer * BLK, BLK), pl.ds(i * BLK, BLK)
                ]


def call(kernel, scalars, arrays, outs, scratch, blocks=()):
    vmem = pl.BlockSpec(memory_space=pltpu.VMEM)
    smem = pl.BlockSpec(memory_space=pltpu.SMEM)
    anywhere = pl.BlockSpec(memory_space=pl.ANY)
    return pl.pallas_call(
        kernel,
        in_specs=[smem] * len(scalars) + [anywhere] * len(arrays) + [vmem] * len(blocks),
        out_specs=[vmem] * len(outs),
        out_shape=[jax.ShapeDtypeStruct(*o) for o in outs],
        scratch_shapes=list(scratch),
        compiler_params=pltpu.CompilerParams(vmem_limit_bytes=VMEM_LIMIT),
    )(*scalars, *arrays, *blocks)


def per_device(root_factor, root_pivots, child_factor, child_pivots, child_block, child_rows):
    row = lax.axis_index("row")
    col = lax.axis_index("col")
    bf16 = jnp.bfloat16
    root_turned, child_turned, right_here = call(
        functools.partial(prepare_kernel, 1),
        (),
        (),
        [((768, BLK), bf16), ((1536, BLK), bf16), ((2304, BLK), bf16)],
        (),
        (
            root_factor.reshape(384, 384),
            root_pivots.reshape(3, BLK),
            child_factor.reshape(512, 256),
            child_pivots.reshape(4, BLK),
            child_block.reshape(384, 256),
        ),
    )
    turned = permute(root_turned, transposed_place)
    right = lax.all_gather(right_here, "row", axis=0, tiled=False)

    rows = child_rows[0].reshape(48, REACH) % BLK
    row_picks = lax.dynamic_index_in_dim(rows.reshape(6, N_ROW, REACH), row, 1, keepdims=False)
    col_picks = lax.dynamic_index_in_dim(rows.reshape(3, N_COL, REACH), col, 1, keepdims=False)
    my_picks = jnp.concatenate([row_picks.reshape(-1), col_picks.reshape(-1)])[:, None]
    other_picks = permute(my_picks, other_half)
    child_turned = lax.optimization_barrier((child_turned, other_picks))[0]
    child_here = permute(child_turned, transposed_place)

    side = jnp.arange(2, dtype=jnp.int32)[:, None]
    classes = jnp.arange(N_ROW, dtype=jnp.int32)[None, :]
    source = side * N_ROW + mixed(classes, row)
    my_x, my_y = col % SIDE, col // SIDE

    def plane_slots(place):
        dx = (place % SIDE - my_x) % SIDE
        dy = (place // SIDE - my_y) % SIDE
        return (dy * SIDE + dx).reshape(-1), (dx * SIDE + dy).reshape(-1)

    root_slots = plane_slots(source)
    offdiag_slots = plane_slots(side * N_ROW + classes)
    slots = source.reshape(-1)
    r = classes[0]
    part_slots = ((r ^ row) & 1) * SIDE + (r // 2 - row // 2) % SIDE
    turned, root_slots, offdiag_slots, slots, part_slots, my_picks, other_picks = lax.optimization_barrier(
        (turned, root_slots, offdiag_slots, slots, part_slots, my_picks, other_picks)
    )
    root_parts = plane_gather(turned[:384], turned[384:])

    partial, theirs, mine = call(
        root_kernel,
        root_slots,
        (*root_parts[0], *root_parts[1], right),
        [((768, 384), bf16), ((192, 384), bf16), ((192, 384), bf16)],
        [
            pltpu.VMEM((N_COL, 384, BLK), bf16),
            pltpu.VMEM((N_COL, 384, BLK), bf16),
            pltpu.VMEM((N_ROW, 768, BLK), bf16),
            pltpu.VMEM((2, 384, 384), jnp.float32),
            pltpu.SemaphoreType.DMA((11,)),
        ],
        (other_picks, my_picks),
    )
    child_here = lax.optimization_barrier((child_here, partial))[0]
    child_left = lax.all_gather(child_here, "col", axis=0, tiled=False)
    theirs = permute(theirs, other_half)
    picked = (mine.astype(jnp.float32) + theirs.astype(jnp.float32)).astype(bf16)
    late = lax.optimization_barrier((partial, picked))[0]
    late = permute(late, other_half)
    (root_inverse,) = call(sum_kernel, (), (), [((2304, BLK), jnp.float32)], (), (partial, late))
    picked_parts = plane_gather(picked[:96], picked[96:])
    offdiag, offdiag_low = call(
        offdiag_kernel,
        offdiag_slots,
        (*picked_parts[0], *picked_parts[1], right),
        [((768, BLK), jnp.float32), ((256, 384), bf16)],
        [
            pltpu.VMEM((N_COL, 96, 384), bf16),
            pltpu.VMEM((N_COL, 96, 384), bf16),
            pltpu.VMEM((N_ROW, 768, BLK), bf16),
            pltpu.VMEM((256, 384), jnp.float32),
            pltpu.SemaphoreType.DMA((11,)),
        ],
    )
    offdiag_low = lax.optimization_barrier((offdiag_low, late))[0]
    line = ring_parts(offdiag_low, along_z, True)
    ready = lax.optimization_barrier((line, root_inverse))[0]
    parts = line + [permute(part, other_core) for part in ready]
    (child_inverse,) = call(
        child_kernel,
        (slots, part_slots),
        (*parts, child_left, right),
        [((1024, BLK), jnp.float32)],
        [
            pltpu.VMEM((N_COL, 1536, BLK), bf16),
            pltpu.VMEM((N_ROW, 768, BLK), bf16),
            pltpu.VMEM((N_ROW, 256, 384), bf16),
            pltpu.VMEM((2, 256, 256), jnp.float32),
            pltpu.SemaphoreType.DMA((13,)),
        ],
    )
    return (
        root_inverse.reshape(6, 1, BLK, 3, 1, BLK),
        offdiag.reshape(child_block.shape),
        child_inverse.reshape(child_factor.shape),
    )


def solution(mesh):
    return jax.shard_map(
        per_device,
        mesh=mesh,
        in_specs=(
            P(None, ("half", "row"), None, None, "col", None),
            P(None, ("half", "row"), None),
            P("half", None, "row", None, None, "col", None),
            P("half", None, "row", None),
            P("half", None, "row", None, None, "col", None),
            P("half", None),
        ),
        out_specs=(
            P(None, "row", None, None, "col", None),
            P("half", None, "row", None, None, "col", None),
            P("half", None, "row", None, None, "col", None),
        ),
        check_vma=False,
    )
```
